128 devices in a mesh: region: 32 (over y, x, z_lo), view: 4 (over z_hi, core).
Axes of the slice: x: 4, y: 4, z: 4 (z_hi: 2, z_lo: 2; z = z_hi * 2 + z_lo), core: 2. Of those that a mesh axis runs over, the one named last changes fastest.
Arguments:
- embeddings: bfloat16 [32768, 768], P(('region', 'view')), may hold values from -6 to 6
- region_ids: int32 [32768], P(('region', 'view')), may hold values from 0 to 16383, as said below
- tile_ids: int32 [32768], P(('region', 'view')), may hold values from 0 to 2047, as said below
- logit_scale: float32 [1], replicated, may hold values from 1.5 to 3
- logit_bias: float32 [1], replicated, may hold values from -7 to -5
Outputs:
- grads: float32 [32768, 768], P(('region', 'view'))
The draws below stay inside these ranges and needn't reach their ends.
Inputs may be any that keep to these rules, and one draw needn't show every extreme that they name: `region_ids`: every region id appears exactly twice, once for each view. `tile_ids`: embeddings with the same region id have the same tile id; every tile holds exactly 8 regions.
All inputs are finite; a program needn't handle non-finite values.
Results may differ from the reference program's by a relative error of at most 0.00075.
Values may be sent and summed in bfloat16 or wider, within the bound.
A program may use at most 64 MiB of HBM per device.

```python
import math
import jax
import jax.numpy as jnp
from jax import lax

D = 768
EMBEDS = 32768


def pairing(key):
    order = jax.random.permutation(key, EMBEDS).astype(jnp.int32)
    region = order // 2
    tiles = jax.random.permutation(jax.random.fold_in(key, 7), EMBEDS // 2).astype(jnp.int32) // 8
    return (region, tiles[region])


def draw_region_ids(key, part):
    shared = pairing(key)
    return shared[0]


def draw_tile_ids(key, part):
    shared = pairing(key)
    return shared[1]


def shard_levels(rng, extent, cuts, smallest, high):
    loudness = 1.0
    for dim, blocks in cuts:
        draws = jax.random.uniform(jax.random.fold_in(jax.random.fold_in(rng, 6), dim), (blocks,), jnp.float32, smallest / len(cuts), high / len(cuts))
        loudness = loudness * jnp.repeat(jnp.exp(draws), extent[dim] // blocks).reshape((-1,) + (1,) * (len(extent) - 1 - dim))
    return loudness


def noise(own_key, dims, width, limit, split=(), held_as=jnp.bfloat16):
    array = jax.random.normal(own_key, dims, jnp.float32) * width
    if len(split) > 0:
        array = shard_levels(own_key, dims, split, -0.22, 0.18) * array
    return jnp.clip(array, min=-limit, max=limit).astype(held_as)


def setup_inputs(seed: int = 0) -> dict:
    splits = jax.random.split(jax.random.key(seed), 6)
    return {
        "embeddings": noise(splits[0], (EMBEDS, D), 1.0, 6.0, ((0, 128),)),
        "region_ids": draw_region_ids(jax.random.fold_in(splits[5], 71), 0),
        "tile_ids": draw_tile_ids(jax.random.fold_in(splits[5], 71), 0),
        "logit_scale": jnp.clip(jax.random.uniform(splits[3], (1,), jnp.float32, 1.5, 3.0), 1.5, 3.0),
        "logit_bias": jnp.clip(jax.random.uniform(splits[4], (1,), jnp.float32, -7.0, -5.0), -7.0, -5.0),
    }


def reference(embeddings, region_ids, tile_ids, logit_scale, logit_bias):
    total = embeddings.shape[0]
    block = math.gcd(total, 1024)
    scale = logit_scale[0] * (1.0 / math.sqrt(D))
    bias = logit_bias[0]
    col_index = jnp.arange(total, dtype=jnp.int32)

    def one_block(start):
        rows = lax.dynamic_slice_in_dim(embeddings, start, block, 0)
        row_ids = lax.dynamic_slice_in_dim(region_ids, start, block, 0)
        row_tiles = lax.dynamic_slice_in_dim(tile_ids, start, block, 0)
        logits = jnp.einsum('qd,kd->qk', rows, embeddings, preferred_element_type=jnp.float32) * scale + bias
        row_index = start + jnp.arange(block, dtype=jnp.int32)
        same = row_ids[:, None] == region_ids[None, :]
        sign = jnp.where(same, 1.0, -1.0).astype(jnp.float32)
        keep = (row_index[:, None] != col_index[None, :]) & (same | (row_tiles[:, None] != tile_ids[None, :]))
        slope = jnp.where(keep, -sign * jax.nn.sigmoid(-sign * logits), 0.0).astype(jnp.bfloat16)
        return jnp.dot(slope, embeddings, preferred_element_type=jnp.float32) * (2.0 * scale)
    starts = jnp.arange(total // block, dtype=jnp.int32) * block
    result = lax.map(one_block, starts)
    return result.reshape(total, embeddings.shape[1])
```

```python
import functools
import math

import jax
import jax.numpy as jnp
from jax import lax
from jax.experimental import pallas as pl
from jax.experimental.pallas import tpu as pltpu
from jax.sharding import PartitionSpec as P

D = 768
B = 256
H = B // 2
MESH = pl.DeviceIdType.MESH
NT = (((1,), (1,)), ((), ()))

SLOTS = [(0, 0), (1, 0), (3, 0), (0, 1), (0, 3), (2, 0), (1, 1), (1, 3)]
SLOTS += [(3, 1), (3, 3), (0, 2), (2, 1), (2, 3), (1, 2), (3, 2), (2, 2)]
SLOT = {rel: k for k, rel in enumerate(SLOTS)}

OPP, UP, DOWN, OWN = 0, B, 2 * B, 3 * B


def wrap(value):
    return lax.rem(value + 4, 4)


def device(x, y, z, core):
    x, y, z = wrap(x), wrap(y), wrap(z)
    return ((y * 4 + x) * 2 + lax.rem(z, 2), lax.div(z, 2) * 2 + core)


def kernel(x_ref, meta_ref, scale_ref, bias_ref, out_ref, keys, rows, acc, key_meta, line_meta, key_ids, row_ids,
           row_tiles, halves, wholes, send, recv):
    region = lax.axis_index("region")
    view = lax.axis_index("view")
    y, x = lax.div(region, 8), lax.rem(lax.div(region, 2), 4)
    z, core = lax.div(view, 2) * 2 + lax.rem(region, 2), lax.rem(view, 2)
    sibling = device(x, y, z, 1 - core)

    def first(step):
        return device(x + (1 - core) * step, y + core * step, z, core)

    def second(step):
        return device(x + core * step, y + (1 - core) * step, z, core)

    def line(step):
        return device(x, y, z + step, core)

    barrier = pltpu.get_barrier_semaphore()
    peers = [sibling] + [go(step) for go in (first, second, line) for step in (1, -1, 2)]
    for peer in peers:
        pl.semaphore_signal(barrier, inc=1, device_id=peer, device_id_type=MESH)
    pl.semaphore_wait(barrier, len(peers))

    copies = {}

    def start(name, src, dst, target):
        index = len(copies)
        copies[name] = pltpu.make_async_remote_copy(
            src_ref=src, dst_ref=dst, send_sem=send.at[index], recv_sem=recv.at[index],
            device_id=target, device_id_type=MESH,
        )
        copies[name].start()

    def arrived(*names):
        for name in names:
            copies[name].wait_recv()

    def slot(rel, whose=0, begin=0, count=B):
        return keys.at[pl.ds((2 * SLOT[rel] + whose) * B + begin, count)]

    def moved(rel, axis, step):
        return tuple((r - step * (i == axis)) % 4 for i, r in enumerate(rel))

    def whole(rel, axis, step):
        start(("w", axis, step, rel), x_ref if rel == (0, 0) else slot(rel), slot(moved(rel, axis, step)),
              (first, second)[axis](step))

    def half(rel, axis, step):
        begin = 0 if step == 1 else H
        start(("h", axis, step, rel), slot(rel, 0, begin, H), slot(moved(rel, axis, step), 0, begin, H),
              (first, second)[axis](step))

    def share(rel):
        start(("s", rel), x_ref if rel == (0, 0) else slot(rel), slot(rel, 1), sibling)

    def shared(*rels):
        arrived(*[("s", rel) for rel in rels])

    def from_whole(axis, *rels):
        for rel in rels:
            step = 1 if rel[axis] == 3 else -1
            arrived(("w", axis, step, moved(rel, axis, -step)))

    def from_halves(axis, rel):
        arrived(("h", axis, 1, moved(rel, axis, -1)), ("h", axis, -1, moved(rel, axis, 1)))

    mine = pl.ds(pl.multiple_of(((y * 4 + x) * 2 + core) * 8, 8), 8)
    chip = pl.ds(pl.multiple_of((y * 4 + x) * 16, 16), 16)
    lane = pl.ds(pl.multiple_of(y * 64, 64), 64)
    key_meta[mine, :] = meta_ref[...]
    start("ms", meta_ref, key_meta.at[mine], sibling)
    start("mu", meta_ref, line_meta.at[pl.ds(16, 8)], line(1))
    start("md", meta_ref, line_meta.at[pl.ds(8, 8)], line(-1))
    start("mo", meta_ref, line_meta.at[pl.ds(0, 8)], line(2))

    for axis in (0, 1):
        for step in (1, -1):
            whole((0, 0), axis, step)
    start("ru", x_ref, rows.at[pl.ds(DOWN, B)], line(1))
    start("rd", x_ref, rows.at[pl.ds(UP, B)], line(-1))
    share((0, 0))

    keys[0:B, :] = x_ref[...]
    rows[OWN:OWN + B, :] = x_ref[...]
    line_meta[24:32, :] = meta_ref[...]
    acc[...] = jnp.zeros_like(acc)

    def beside(step):
        return device(x + step, y, z, core)

    def across(step):
        return device(x, y + step, z, core)

    arrived("ms")
    for step in (1, -1, 2):
        start(("mx", step), key_meta.at[chip], key_meta.at[chip], beside(step))
    arrived(("mx", 1), ("mx", -1), ("mx", 2))
    for step in (1, -1, 2):
        start(("my", step), key_meta.at[lane], key_meta.at[lane], across(step))
    arrived("mu", "md", "mo")
    for block in range(4):
        for part in range(2):
            at = pl.ds(block * B + part * H, H)
            row = block * 8 + part
            row_ids[at, :] = jnp.broadcast_to(line_meta[row:row + 1, :], (H, H)).T
            row_tiles[at, :] = jnp.broadcast_to(line_meta[row + 2:row + 3, :], (H, H)).T
    arrived(("my", 1), ("my", -1), ("my", 2))
    for k, (a, b) in enumerate(SLOTS):
        for whose in range(2):
            owner = core + whose - 2 * core * whose
            kx = wrap(x + (1 - owner) * a + owner * b)
            ky = wrap(y + owner * a + (1 - owner) * b)
            tile = key_meta[pl.ds(pl.multiple_of(((ky * 4 + kx) * 2 + owner) * 8, 8), 8), :]
            for part in range(2):
                at = pl.ds((2 * k + whose) * B + part * H, H)
                key_ids[0:1, at] = tile[part:part + 1, :]
                key_ids[1:2, at] = tile[part + 2:part + 3, :]

    half_scale = scale_ref[0] * (0.5 / math.sqrt(D))
    half_bias = bias_ref[0] * 0.5

    def work(row, count, k, ks, diagonal=False):
        at, cols = pl.ds(row, count), pl.ds(2 * B * k, 2 * B * ks)
        block = keys[cols, :]
        logits = lax.dot_general(rows[at, :], block, NT, preferred_element_type=jnp.float32)
        curve = jnp.tanh(logits * half_scale + half_bias)
        same = row_ids[at, :][:, 0:1] == key_ids[0:1, cols]
        if diagonal:
            same &= lax.broadcasted_iota(jnp.int32, curve.shape, 0) != lax.broadcasted_iota(jnp.int32, curve.shape, 1)
        near = row_tiles[at, :][:, 0:1] == key_ids[1:2, cols]
        slope = curve + jnp.where(same, -1.0, 1.0)
        slope = jnp.where(near & ~same, 0.0, slope).astype(jnp.bfloat16)
        acc[at, :] += jnp.dot(slope, block, preferred_element_type=jnp.float32)

    shared((0, 0))
    work(OWN, B, 0, 1, diagonal=True)

    from_whole(0, (1, 0), (3, 0))
    for step in (1, -1):
        half(((3 if step == 1 else 1), 0), 0, step)
        whole((1, 0), 1, step)
        whole((3, 0), 1, step)
    from_whole(1, (0, 1), (0, 3))
    for step in (1, -1):
        half((0, 3 if step == 1 else 1), 1, step)
    arrived("ru", "rd")
    start("ou", rows.at[pl.ds(DOWN, H)], rows.at[pl.ds(OPP, H)], line(1))
    start("od", rows.at[pl.ds(UP + H, H)], rows.at[pl.ds(OPP + H, H)], line(-1))
    for rel in SLOTS[1:5]:
        share(rel)
    work(UP, 2 * B, 0, 1)
    shared(*SLOTS[1:5])
    work(UP, 3 * B, 1, 4)

    from_halves(0, (2, 0))
    for step in (1, -1):
        whole((2, 0), 1, step)
    from_whole(1, (1, 1), (1, 3))
    for step in (1, -1):
        half((1, 3 if step == 1 else 1), 1, step)
    for rel in SLOTS[5:8]:
        share(rel)
    arrived("ou", "od")
    work(OPP, B, 0, 5)
    shared(*SLOTS[5:8])
    work(OPP, 2 * B, 5, 3)

    from_whole(1, (3, 1), (3, 3))
    for step in (1, -1):
        half((3, 3 if step == 1 else 1), 1, step)
    from_halves(1, (0, 2))
    for rel in SLOTS[8:11]:
        share(rel)
    work(DOWN, 2 * B, 5, 3)
    shared(*SLOTS[8:11])
    work(OPP, 2 * B, 8, 3)

    from_whole(1, (2, 1), (2, 3))
    for step in (1, -1):
        half((2, 3 if step == 1 else 1), 1, step)
    for rel in SLOTS[11:13]:
        share(rel)
    work(DOWN, 2 * B, 8, 3)
    shared(*SLOTS[11:13])
    work(OPP, 2 * B, 11, 2)
    work(DOWN, 2 * B, 11, 2)

    from_halves(1, (1, 2))
    share((1, 2))
    from_halves(1, (3, 2))
    share((3, 2))
    from_halves(1, (2, 2))
    share((2, 2))
    shared(*SLOTS[13:16])
    work(OPP, B, 13, 3)
    start("hu", acc.at[pl.ds(OPP, H)], halves.at[0], line(1))
    start("hd", acc.at[pl.ds(OPP + H, H)], halves.at[1], line(-1))
    work(UP, B, 13, 3)
    work(DOWN, B, 13, 3)
    arrived("hu", "hd")
    acc[UP:UP + H, :] += halves[0]
    start("gu", acc.at[pl.ds(UP, B)], wholes.at[0], line(1))
    acc[DOWN + H:DOWN + B, :] += halves[1]
    start("gd", acc.at[pl.ds(DOWN, B)], wholes.at[1], line(-1))
    work(OWN, B, 13, 3)
    arrived("gu", "gd")
    out_ref[...] = (acc[OWN:OWN + B, :] + wholes[0] + wholes[1]) * (2.0 * half_scale)
    for copy in copies.values():
        copy.wait_send()


COPIES = 64


def local(embeddings, region_ids, tile_ids, logit_scale, logit_bias):
    meta = jnp.concatenate(
        [region_ids.reshape(2, H), tile_ids.reshape(2, H), jnp.zeros((4, H), jnp.int32)], axis=0
    )
    vmem, smem = pl.BlockSpec(memory_space=pltpu.VMEM), pl.BlockSpec(memory_space=pltpu.SMEM)
    return pl.pallas_call(
        kernel,
        out_shape=jax.ShapeDtypeStruct((B, D), jnp.float32),
        in_specs=[vmem, vmem, smem, smem],
        out_specs=vmem,
        scratch_shapes=[
            pltpu.VMEM((32 * B, D), jnp.bfloat16),
            pltpu.VMEM((4 * B, D), jnp.bfloat16),
            pltpu.VMEM((4 * B, D), jnp.float32),
            pltpu.VMEM((B, H), jnp.int32),
            pltpu.VMEM((32, H), jnp.int32),
            pltpu.VMEM((8, 32 * B), jnp.int32),
            pltpu.VMEM((4 * B, H), jnp.int32),
            pltpu.VMEM((4 * B, H), jnp.int32),
            pltpu.VMEM((2, H, D), jnp.float32),
            pltpu.VMEM((2, B, D), jnp.float32),
            pltpu.SemaphoreType.DMA((COPIES,)),
            pltpu.SemaphoreType.DMA((COPIES,)),
        ],
        compiler_params=pltpu.CompilerParams(
            collective_id=0, has_side_effects=True, vmem_limit_bytes=56 * 1024 * 1024
        ),
        name="pair_gradients",
    )(embeddings, meta, logit_scale, logit_bias)


def solution(mesh):
    placed = (P(("region", "view"), None), P(("region", "view")), P(("region", "view")), P(), P())
    return jax.shard_map(
        local, mesh=mesh, in_specs=placed, out_specs=P(("region", "view"), None), check_vma=False
    )
```

```python
import functools
import math

import jax
import jax.numpy as jnp
from jax import lax
from jax.experimental import pallas as pl
from jax.experimental.pallas import tpu as pltpu
from jax.sharding import PartitionSpec as P

D = 768
B = 256
H = B // 2
MESH = pl.DeviceIdType.MESH
NT = (((1,), (1,)), ((), ()))

SLOTS = [(0, 0), (1, 0), (3, 0), (0, 1), (0, 3), (2, 0), (1, 1), (1, 3)]
SLOTS += [(3, 1), (3, 3), (0, 2), (2, 1), (2, 3), (1, 2), (3, 2), (2, 2)]
SLOT = {rel: k for k, rel in enumerate(SLOTS)}

OPP, UP, DOWN, OWN = 0, B, 2 * B, 3 * B


def wrap(value):
    return lax.rem(value + 4, 4)


def device(x, y, z, core):
    x, y, z = wrap(x), wrap(y), wrap(z)
    return ((y * 4 + x) * 2 + lax.rem(z, 2), lax.div(z, 2) * 2 + core)


def kernel(x_ref, ids_ref, tiles_ref, scale_ref, bias_ref, out_ref, keys, rows, acc, key_meta, line_meta, key_ids,
           row_ids, row_tiles, coded, coded_top, landed, landed_top, local_sem, send, recv):
    region = lax.axis_index("region")
    view = lax.axis_index("view")
    y, x = lax.div(region, 8), lax.rem(lax.div(region, 2), 4)
    z, core = lax.div(view, 2) * 2 + lax.rem(region, 2), lax.rem(view, 2)
    sibling = device(x, y, z, 1 - core)

    def first(step):
        return device(x + (1 - core) * step, y + core * step, z, core)

    def second(step):
        return device(x + core * step, y + (1 - core) * step, z, core)

    def line(step):
        return device(x, y, z + step, core)

    fetch = pltpu.make_async_copy(x_ref, keys.at[pl.ds(0, B)], local_sem)
    fetch.start()
    barrier = pltpu.get_barrier_semaphore()
    peers = [sibling] + [go(step) for go in (first, second, line) for step in (1, -1)]
    for peer in peers:
        pl.semaphore_signal(barrier, inc=1, device_id=peer, device_id_type=MESH)
    for part in range(2):
        for held in (key_meta.at[0, part], line_meta.at[3, part]):
            held[0:1, :] = ids_ref[part:part + 1, :]
            held[1:2, :] = tiles_ref[part:part + 1, :]
    fetch.wait()
    pl.semaphore_wait(barrier, len(peers))

    copies = {}

    def start(name, src, dst, target):
        index = len(copies)
        copies[name] = pltpu.make_async_remote_copy(
            src_ref=src, dst_ref=dst, send_sem=send.at[index], recv_sem=recv.at[index],
            device_id=target, device_id_type=MESH,
        )
        copies[name].start()

    def arrived(*names):
        for name in names:
            copies[name].wait_recv()

    def slot(rel, whose=0, begin=0, count=B):
        return keys.at[pl.ds((2 * SLOT[rel] + whose) * B + begin, count)]

    def meta(rel, whose=0):
        return key_meta.at[2 * SLOT[rel] + whose]

    def moved(rel, axis, step):
        return tuple((r - step * (i == axis)) % 4 for i, r in enumerate(rel))

    def whole(rel, axis, step):
        target = (first, second)[axis](step)
        to = moved(rel, axis, step)
        start(("mw", axis, step, rel), meta(rel), meta(to), target)
        start(("w", axis, step, rel), slot(rel), slot(to), target)

    def half(rel, axis, step):
        target = (first, second)[axis](step)
        to = moved(rel, axis, step)
        begin = 0 if step == 1 else H
        if step == 1:
            start(("mh", axis, rel), meta(rel), meta(to), target)
        start(("h", axis, step, rel), slot(rel, 0, begin, H), slot(to, 0, begin, H), target)

    def share(*rels):
        for rel in rels:
            start(("ms", rel), meta(rel), meta(rel, 1), sibling)
            start(("s", rel), slot(rel), slot(rel, 1), sibling)

    def shared(*rels):
        for rel in rels:
            arrived(("ms", rel), ("s", rel))
        for rel in rels:
            for whose in range(2):
                at = 2 * SLOT[rel] + whose
                for part in range(2):
                    key_ids[0:2, pl.ds(at * B + part * H, H)] = key_meta[at, part]

    def from_whole(axis, *rels):
        for rel in rels:
            step = 1 if rel[axis] == 3 else -1
            arrived(("mw", axis, step, moved(rel, axis, -step)), ("w", axis, step, moved(rel, axis, -step)))

    def from_halves(axis, rel):
        arrived(("mh", axis, moved(rel, axis, -1)))
        arrived(("h", axis, 1, moved(rel, axis, -1)), ("h", axis, -1, moved(rel, axis, 1)))

    for axis in (0, 1):
        for step in (1, -1):
            whole((0, 0), axis, step)
    start("mu", line_meta.at[3], line_meta.at[2], line(1))
    start("md", line_meta.at[3], line_meta.at[1], line(-1))
    start("ru", keys.at[pl.ds(0, B)], rows.at[pl.ds(DOWN, B)], line(1))
    start("rd", keys.at[pl.ds(0, B)], rows.at[pl.ds(UP, B)], line(-1))
    share((0, 0))
    rows[OWN:OWN + B, :] = keys[0:B, :]
    acc[...] = jnp.zeros_like(acc)

    def label_rows(*blocks):
        for block in blocks:
            for part in range(2):
                at = pl.ds(block * B + part * H, H)
                held = line_meta[block, part]
                row_ids[at, :] = jnp.broadcast_to(held[0:1, :], (H, H)).T
                row_tiles[at, :] = jnp.broadcast_to(held[1:2, :], (H, H)).T

    half_scale = scale_ref[0] * (0.5 / math.sqrt(D))
    half_bias = bias_ref[0] * 0.5

    def work(row, count, k, ks, diagonal=False):
        at, cols = pl.ds(row, count), pl.ds(2 * B * k, 2 * B * ks)
        block = keys[cols, :]
        logits = lax.dot_general(rows[at, :], block, NT, preferred_element_type=jnp.float32)
        curve = jnp.tanh(logits * half_scale + half_bias)
        same = row_ids[at, :][:, 0:1] == key_ids[0:1, cols]
        if diagonal:
            same &= lax.broadcasted_iota(jnp.int32, curve.shape, 0) != lax.broadcasted_iota(jnp.int32, curve.shape, 1)
        near = row_tiles[at, :][:, 0:1] == key_ids[1:2, cols]
        slope = curve + jnp.where(same, -1.0, 1.0)
        slope = jnp.where(near & ~same, 0.0, slope).astype(jnp.bfloat16)
        acc[at, :] += jnp.dot(slope, block, preferred_element_type=jnp.float32)

    def pass_on(piece, row, step):
        sums = acc[pl.ds(row, H), :].reshape(H // 8, 8, D)
        top = jnp.maximum(jnp.max(jnp.abs(sums), axis=0), 1e-30)
        coded_top[piece] = top
        code = jnp.floor(sums * (32767.0 / top)[None] + 0.5).astype(jnp.int32)
        coded[piece] = code.reshape(H, D).astype(jnp.int16)
        start(("t", piece), coded_top.at[piece], landed_top.at[piece], line(step))
        start(("q", piece), coded.at[piece], landed.at[piece], line(step))

    def take_in(piece, row):
        arrived(("t", piece), ("q", piece))
        sums = landed[piece].astype(jnp.int32).astype(jnp.float32).reshape(H // 8, 8, D)
        sums = sums * (landed_top[piece] * (1.0 / 32767.0))[None]
        acc[pl.ds(row, H), :] += sums.reshape(H, D)

    label_rows(3)
    shared((0, 0))
    work(OWN, B, 0, 1, diagonal=True)

    from_whole(0, (1, 0), (3, 0))
    for step in (1, -1):
        half(((3 if step == 1 else 1), 0), 0, step)
        whole((1, 0), 1, step)
        whole((3, 0), 1, step)
    from_whole(1, (0, 1), (0, 3))
    for step in (1, -1):
        half((0, 3 if step == 1 else 1), 1, step)
    share(*SLOTS[1:5])
    arrived("mu", "md", "ru", "rd")
    start("mo", line_meta.at[2], line_meta.at[0], line(1))
    start("ou", rows.at[pl.ds(DOWN, H)], rows.at[pl.ds(OPP, H)], line(1))
    start("od", rows.at[pl.ds(UP + H, H)], rows.at[pl.ds(OPP + H, H)], line(-1))
    label_rows(1, 2)
    work(UP, 2 * B, 0, 1)
    shared(*SLOTS[1:5])
    work(UP, 2 * B, 1, 4)

    arrived("mo", "ou", "od")
    label_rows(0)
    from_halves(0, (2, 0))
    for step in (1, -1):
        whole((2, 0), 1, step)
    work(OPP, B, 0, 5)
    from_whole(1, (1, 1), (1, 3))
    for step in (1, -1):
        half((1, 3 if step == 1 else 1), 1, step)
    share(*SLOTS[5:8])
    work(OWN, B, 1, 4)
    shared(*SLOTS[5:8])
    work(UP, 2 * B, 5, 3)

    from_whole(1, (3, 1), (3, 3))
    for step in (1, -1):
        half((3, 3 if step == 1 else 1), 1, step)
    from_halves(1, (0, 2))
    share(*SLOTS[8:11])
    work(OPP, B, 5, 3)
    shared(*SLOTS[8:11])
    work(UP, 2 * B, 8, 3)

    from_whole(1, (2, 1), (2, 3))
    for step in (1, -1):
        half((2, 3 if step == 1 else 1), 1, step)
    share(*SLOTS[11:13])
    work(OPP, B, 8, 3)
    shared(*SLOTS[11:13])
    work(UP, 2 * B, 11, 2)

    from_halves(1, (1, 2))
    from_halves(1, (3, 2))
    share(*SLOTS[13:15])
    work(OPP, B, 11, 2)
    shared(*SLOTS[13:15])
    work(UP, 2 * B, 13, 2)

    from_halves(1, (2, 2))
    share((2, 2))
    work(OPP, B, 13, 2)
    shared((2, 2))
    work(OPP, B, 15, 1)
    pass_on(0, OPP, 1)
    pass_on(1, OPP + H, -1)
    work(UP, 2 * B, 15, 1)
    pass_on(2, UP + H, 1)
    pass_on(3, DOWN, -1)
    work(OWN, B, 5, 6)
    take_in(0, UP)
    pass_on(4, UP, 1)
    take_in(1, DOWN + H)
    pass_on(5, DOWN + H, -1)
    work(OWN, B, 11, 5)
    take_in(2, OWN + H)
    take_in(3, OWN)
    take_in(4, OWN)
    take_in(5, OWN + H)
    out_ref[...] = acc[OWN:OWN + B, :]
    for copy in copies.values():
        copy.wait_send()


COPIES = 112


def local(embeddings, region_ids, tile_ids, logit_scale, logit_bias):
    vmem, smem = pl.BlockSpec(memory_space=pltpu.VMEM), pl.BlockSpec(memory_space=pltpu.SMEM)
    sums = pl.pallas_call(
        kernel,
        out_shape=jax.ShapeDtypeStruct((B, D), jnp.float32),
        in_specs=[pl.BlockSpec(memory_space=pl.ANY), vmem, vmem, smem, smem],
        out_specs=vmem,
        scratch_shapes=[
            pltpu.VMEM((32 * B, D), jnp.bfloat16),
            pltpu.VMEM((4 * B, D), jnp.bfloat16),
            pltpu.VMEM((4 * B, D), jnp.float32),
            pltpu.VMEM((32, 2, 2, H), jnp.int32),
            pltpu.VMEM((4, 2, 2, H), jnp.int32),
            pltpu.VMEM((8, 32 * B), jnp.int32),
            pltpu.VMEM((4 * B, H), jnp.int32),
            pltpu.VMEM((4 * B, H), jnp.int32),
            pltpu.VMEM((6, H, D), jnp.int16),
            pltpu.VMEM((6, 8, D), jnp.float32),
            pltpu.VMEM((6, H, D), jnp.int16),
            pltpu.VMEM((6, 8, D), jnp.float32),
            pltpu.SemaphoreType.DMA,
            pltpu.SemaphoreType.DMA((COPIES,)),
            pltpu.SemaphoreType.DMA((COPIES,)),
        ],
        compiler_params=pltpu.CompilerParams(
            collective_id=0, has_side_effects=True, vmem_limit_bytes=56 * 1024 * 1024
        ),
        name="pair_gradients",
    )(embeddings, region_ids.reshape(2, H), tile_ids.reshape(2, H), logit_scale, logit_bias)
    return sums * (logit_scale[0] * (1.0 / math.sqrt(D)))


def solution(mesh):
    placed = (P(("region", "view"), None), P(("region", "view")), P(("region", "view")), P(), P())
    return jax.shard_map(
        local, mesh=mesh, in_specs=placed, out_specs=P(("region", "view"), None), check_vma=False
    )
```

```python
import functools
import math

import jax
import jax.numpy as jnp
from jax import lax
from jax.experimental import pallas as pl
from jax.experimental.pallas import tpu as pltpu
from jax.sharding import PartitionSpec as P

D = 768
B = 256
H = B // 2
MESH = pl.DeviceIdType.MESH
NT = (((1,), (1,)), ((), ()))

SLOTS = [(0, 0), (1, 0), (3, 0), (0, 1), (0, 3), (2, 0), (0, 2), (1, 1)]
SLOTS += [(1, 3), (3, 1), (3, 3), (2, 1), (2, 3), (1, 2), (3, 2), (2, 2)]
SLOT = {rel: k for k, rel in enumerate(SLOTS)}

OPP, UP, DOWN, OWN = (0, H), (B, 2 * B), (B + H, 2 * B + H), (3 * B, 3 * B + H)
LINE = (OPP, UP, DOWN, OWN)


def place(k, whose, begin=0):
    if 1 <= k <= 4:
        return 2 * B + begin * 8 + (k - 1) * B + whose * H
    return (2 * k + whose) * B + begin


def wrap(value):
    return lax.rem(value + 4, 4)


def device(x, y, z, core):
    x, y, z = wrap(x), wrap(y), wrap(z)
    return ((y * 4 + x) * 2 + lax.rem(z, 2), lax.div(z, 2) * 2 + core)


def kernel(x_ref, ids_ref, tiles_ref, scale_ref, bias_ref, out_ref, own_ids, keys, rows, acc, key_meta, line_meta,
           key_ids, row_ids, row_tiles, coded, coded_top, landed, landed_top, local_sem, send, recv):
    region = lax.axis_index("region")
    view = lax.axis_index("view")
    y, x = lax.div(region, 8), lax.rem(lax.div(region, 2), 4)
    z, core = lax.div(view, 2) * 2 + lax.rem(region, 2), lax.rem(view, 2)
    sibling = device(x, y, z, 1 - core)

    def first(step):
        return device(x + (1 - core) * step, y + core * step, z, core)

    def second(step):
        return device(x + core * step, y + (1 - core) * step, z, core)

    def line(step):
        return device(x, y, z + step, core)

    fetches = [
        pltpu.make_async_copy(x_ref, keys.at[pl.ds(0, B)], local_sem.at[0]),
        pltpu.make_async_copy(ids_ref, own_ids.at[0], local_sem.at[1]),
        pltpu.make_async_copy(tiles_ref, own_ids.at[1], local_sem.at[2]),
    ]
    for fetch in fetches:
        fetch.start()
    barrier = pltpu.get_barrier_semaphore()
    peers = [sibling] + [go(step) for go in (first, second, line) for step in (1, -1)]
    for peer in peers:
        pl.semaphore_signal(barrier, inc=1, device_id=peer, device_id_type=MESH)
    for fetch in fetches:
        fetch.wait()
    for part in range(2):
        for held in (key_meta.at[0, part], line_meta.at[3, part]):
            held[0:1, :] = own_ids[0, part:part + 1, :]
            held[1:2, :] = own_ids[1, part:part + 1, :]
    pl.semaphore_wait(barrier, len(peers))

    copies = {}

    def start(name, src, dst, target):
        index = len(copies)
        copies[name] = pltpu.make_async_remote_copy(
            src_ref=src, dst_ref=dst, send_sem=send.at[index], recv_sem=recv.at[index],
            device_id=target, device_id_type=MESH,
        )
        copies[name].start()

    def arrived(*names):
        for name in names:
            copies[name].wait_recv()

    def slot(rel, whose=0, begin=0, count=B):
        return keys.at[pl.ds(place(SLOT[rel], whose, begin), count)]

    def meta(rel, whose=0):
        return key_meta.at[2 * SLOT[rel] + whose]

    def moved(rel, axis, step):
        return tuple((r - step * (i == axis)) % 4 for i, r in enumerate(rel))

    def ids_on(rel, axis, step):
        start(("m", axis, step, rel), meta(rel), meta(moved(rel, axis, step)), (first, second)[axis](step))

    def send_on(rel, axis, step, part=None):
        begin, count = (0, B) if part is None else (part * H, H)
        start(("w", axis, step, rel, part), slot(rel, 0, begin, count),
              slot(moved(rel, axis, step), 0, begin, count), (first, second)[axis](step))

    def came(axis, rel, part=None):
        if rel[axis] == 2:
            step = 1 if part == 0 else -1
        else:
            step = 1 if rel[axis] == 3 else -1
        arrived(("w", axis, step, moved(rel, axis, -step), part))

    def ids_came(axis, *rels):
        for rel in rels:
            step = -1 if rel[axis] == 1 else 1
            arrived(("m", axis, step, moved(rel, axis, -step)))

    def share(rel, part=None):
        begin, count = (0, B) if part is None else (part * H, H)
        start(("s", rel, part), slot(rel, 0, begin, count), slot(rel, 1, begin, count), sibling)

    def share_ids(*rels):
        for rel in rels:
            start(("ms", rel), meta(rel), meta(rel, 1), sibling)

    def shared(*wanted):
        for want in wanted:
            rel, parts = (want[0], (want[1],)) if isinstance(want[0], tuple) else (want, (0, 1))
            if 0 in parts:
                arrived(("ms", rel))
            arrived(*[("s", rel, part) for part in (*parts, None) if ("s", rel, part) in copies])
            for whose in range(2):
                at = 2 * SLOT[rel] + whose
                for part in parts:
                    key_ids[0:2, pl.ds(place(SLOT[rel], whose, part * H), H)] = key_meta[at, part]

    here = (0, 0)
    for axis in (0, 1):
        for step in (1, -1):
            ids_on(here, axis, step)
    start("mu", line_meta.at[3], line_meta.at[2], line(1))
    start("md", line_meta.at[3], line_meta.at[1], line(-1))
    for part in range(2):
        for axis in (0, 1):
            for step in (1, -1):
                send_on(here, axis, step, part)
        at = pl.ds(part * H, H)
        start(("ru", part), keys.at[at], rows.at[pl.ds(DOWN[part], H)], line(1))
        start(("rd", part), keys.at[at], rows.at[pl.ds(UP[part], H)], line(-1))
    share_ids(here)
    share(here)
    rows[OWN[0]:OWN[0] + B, :] = keys[0:B, :]
    acc[...] = jnp.zeros_like(acc)

    def label_rows(*blocks):
        for block in blocks:
            for part in range(2):
                at = pl.ds(LINE[block][part], H)
                held = line_meta[block, part]
                row_ids[at, :] = jnp.broadcast_to(held[0:1, :], (H, H)).T
                row_tiles[at, :] = jnp.broadcast_to(held[1:2, :], (H, H)).T

    half_scale = scale_ref[0] * (0.5 / math.sqrt(D))
    half_bias = bias_ref[0] * 0.5

    def work(row, begin, end, diagonal=False):
        at, cols = pl.ds(row, B), pl.ds(begin, end - begin)
        block = keys[cols, :]
        logits = lax.dot_general(rows[at, :], block, NT, preferred_element_type=jnp.float32)
        curve = jnp.tanh(logits * half_scale + half_bias)
        same = row_ids[at, :][:, 0:1] == key_ids[0:1, cols]
        if diagonal:
            same &= lax.broadcasted_iota(jnp.int32, curve.shape, 0) != lax.broadcasted_iota(jnp.int32, curve.shape, 1)
        near = row_tiles[at, :][:, 0:1] == key_ids[1:2, cols]
        slope = curve + jnp.where(same, -1.0, 1.0)
        slope = jnp.where(near & ~same, 0.0, slope).astype(jnp.bfloat16)
        acc[at, :] += jnp.dot(slope, block, preferred_element_type=jnp.float32)

    def pass_on(piece, row, step):
        sums = acc[pl.ds(row, H), :].reshape(H // 8, 8, D)
        top = jnp.maximum(jnp.max(jnp.abs(sums), axis=0), 1e-30)
        coded_top[piece] = top
        code = jnp.floor(sums * (32767.0 / top)[None] + 0.5).astype(jnp.int32)
        coded[piece] = code.reshape(H, D).astype(jnp.int16)
        start(("t", piece), coded_top.at[piece], landed_top.at[piece], line(step))
        start(("q", piece), coded.at[piece], landed.at[piece], line(step))

    def take_in(piece, row):
        arrived(("t", piece), ("q", piece))
        sums = landed[piece].astype(jnp.int32).astype(jnp.float32).reshape(H // 8, 8, D)
        sums = sums * (landed_top[piece] * (1.0 / 32767.0))[None]
        acc[pl.ds(row, H), :] += sums.reshape(H, D)

    def pair(k):
        return SLOTS[k], SLOTS[k + 1]

    def two_hops(rel):
        ids_came(1, rel)
        share_ids(rel)
        for part in range(2):
            came(1, rel, part)
            share(rel, part)

    def beside(rel):
        up, down = (rel, 3), (rel, 1)
        ids_came(1, up, down)
        ids_on(up, 1, 1)
        parts = [None] if rel == 2 else [0, 1]
        for part in parts:
            came(1, up, part)
        send_on(up, 1, 1, 0)
        for part in parts:
            came(1, down, part)
        send_on(down, 1, -1, 1)
        share_ids(down, up)
        share(down)
        share(up)

    def unit(k):
        return 2 * B * k

    opp, near, far, own = 0, B, 2 * B, 3 * B
    near_keys, far_keys = unit(3), unit(5)

    label_rows(3)
    shared(here)
    work(own, 0, unit(1), diagonal=True)

    ids_came(0, *pair(1))
    for rel in pair(1):
        came(0, rel, 0)
    send_on((3, 0), 0, 1, 0)
    for rel in pair(1):
        for step in (1, -1):
            ids_on(rel, 1, step)
            send_on(rel, 1, step, 0)
    ids_on((3, 0), 0, 1)
    ids_came(1, *pair(3))
    for rel in pair(3):
        came(1, rel, 0)
    ids_on((0, 3), 1, 1)
    send_on((0, 3), 1, 1, 0)
    share_ids(*SLOTS[1:5])
    for rel in SLOTS[1:5]:
        share(rel, 0)
    arrived("mu", "md")
    start("mo", line_meta.at[2], line_meta.at[0], line(1))
    arrived(("ru", 0), ("rd", 0))
    start("ou", rows.at[pl.ds(DOWN[0], H)], rows.at[pl.ds(OPP[0], H)], line(1))
    label_rows(1, 2)
    shared(*[(rel, 0) for rel in SLOTS[1:5]])
    work(near, 0, near_keys)

    for rel in pair(1):
        came(0, rel, 1)
    send_on((1, 0), 0, -1, 1)
    for rel in pair(3):
        came(1, rel, 1)
    send_on((0, 1), 1, -1, 1)
    for rel in pair(1):
        for step in (1, -1):
            send_on(rel, 1, step, 1)
    for rel in SLOTS[1:5]:
        share(rel, 1)
    arrived(("ru", 1), ("rd", 1))
    start("od", rows.at[pl.ds(UP[1], H)], rows.at[pl.ds(OPP[1], H)], line(-1))
    work(own, unit(1), near_keys)
    shared(*[(rel, 1) for rel in SLOTS[1:5]])
    work(near, near_keys, far_keys)
    work(far, 0, far_keys)

    arrived("mo", "ou", "od")
    label_rows(0)
    ids_came(0, (2, 0))
    for part in range(2):
        came(0, (2, 0), part)
    for step in (1, -1):
        ids_on((2, 0), 1, step)
        send_on((2, 0), 1, step)
    share_ids((2, 0))
    share((2, 0))
    work(opp, 0, far_keys)
    two_hops((0, 2))
    work(own, near_keys, far_keys)
    beside(1)

    def others(k):
        for row in (opp, near, far):
            work(row, unit(k), unit(k + 2))

    shared(*pair(5))
    others(5)
    beside(3)
    shared(*pair(7))
    others(7)
    shared(*pair(9))
    others(9)
    beside(2)
    work(own, unit(5), unit(9))
    two_hops((1, 2))
    two_hops((3, 2))
    shared(*pair(11))
    others(11)
    two_hops((2, 2))
    shared(*pair(13))
    work(opp, unit(13), unit(15))
    shared((2, 2))

    work(opp, unit(15), unit(16))
    pass_on(0, OPP[0], 1)
    pass_on(1, OPP[1], -1)
    work(near, unit(13), unit(16))
    work(far, unit(13), unit(16))
    pass_on(2, UP[1], 1)
    pass_on(3, DOWN[0], -1)
    work(own, unit(9), unit(13))
    work(own, unit(13), unit(16))
    take_in(0, UP[0])
    pass_on(4, UP[0], 1)
    take_in(1, DOWN[1])
    pass_on(5, DOWN[1], -1)
    take_in(2, OWN[1])
    take_in(3, OWN[0])
    take_in(4, OWN[0])
    take_in(5, OWN[1])
    out_ref[...] = acc[own:own + B, :]
    for copy in copies.values():
        copy.wait_send()


COPIES = 128


def local(embeddings, region_ids, tile_ids, logit_scale, logit_bias):
    hbm, vmem, smem = (pl.BlockSpec(memory_space=space) for space in (pltpu.HBM, pltpu.VMEM, pltpu.SMEM))
    sums = pl.pallas_call(
        kernel,
        out_shape=jax.ShapeDtypeStruct((B, D), jnp.float32),
        in_specs=[hbm, hbm, hbm, smem, smem],
        out_specs=vmem,
        scratch_shapes=[
            pltpu.VMEM((2, 2, H), jnp.int32),
            pltpu.VMEM((32 * B, D), jnp.bfloat16),
            pltpu.VMEM((4 * B, D), jnp.bfloat16),
            pltpu.VMEM((4 * B, D), jnp.float32),
            pltpu.VMEM((32, 2, 2, H), jnp.int32),
            pltpu.VMEM((4, 2, 2, H), jnp.int32),
            pltpu.VMEM((8, 32 * B), jnp.int32),
            pltpu.VMEM((4 * B, H), jnp.int32),
            pltpu.VMEM((4 * B, H), jnp.int32),
            pltpu.VMEM((6, H, D), jnp.int16),
            pltpu.VMEM((6, 8, D), jnp.float32),
            pltpu.VMEM((6, H, D), jnp.int16),
            pltpu.VMEM((6, 8, D), jnp.float32),
            pltpu.SemaphoreType.DMA((3,)),
            pltpu.SemaphoreType.DMA((COPIES,)),
            pltpu.SemaphoreType.DMA((COPIES,)),
        ],
        compiler_params=pltpu.CompilerParams(
            collective_id=0, has_side_effects=True, vmem_limit_bytes=36 * 1024 * 1024
        ),
        name="pair_gradients",
    )(embeddings, region_ids.reshape(2, H), tile_ids.reshape(2, H), logit_scale, logit_bias)
    return sums * (logit_scale[0] * (1.0 / math.sqrt(D)))


def solution(mesh):
    placed = (P(("region", "view"), None), P(("region", "view")), P(("region", "view")), P(), P())
    return jax.shard_map(
        local, mesh=mesh, in_specs=placed, out_specs=P(("region", "view"), None), check_vma=False
    )
```

```python
import functools
import math

import jax
import jax.numpy as jnp
from jax import lax
from jax.experimental import pallas as pl
from jax.experimental.pallas import tpu as pltpu
from jax.sharding import PartitionSpec as P

D = 768
B = 256
H = B // 2
MESH = pl.DeviceIdType.MESH
NT = (((1,), (1,)), ((), ()))

SLOTS = [(0, 0), (1, 0), (3, 0), (0, 1), (0, 3), (2, 0), (1, 1), (1, 3)]
SLOTS += [(3, 1), (3, 3), (2, 1), (2, 3), (0, 2), (1, 2), (3, 2), (2, 2)]
SLOT = {rel: k for k, rel in enumerate(SLOTS)}

OPP, UP, DOWN, OWN = (0, H), (B, 2 * B), (B + H, 2 * B + H), (3 * B, 3 * B + H)
LINE = (OPP, UP, DOWN, OWN)


def place(k, whose, begin=0):
    if 1 <= k <= 4:
        return 2 * B + begin * 8 + (k - 1) * B + whose * H
    return (2 * k + whose) * B + begin


def wrap(value):
    return lax.rem(value + 4, 4)


def device(x, y, z, core):
    x, y, z = wrap(x), wrap(y), wrap(z)
    return ((y * 4 + x) * 2 + lax.rem(z, 2), lax.div(z, 2) * 2 + core)


def kernel(x_ref, ids_ref, tiles_ref, scale_ref, bias_ref, out_ref, own_ids, keys, rows, acc, key_meta, line_meta,
           key_ids, row_ids, row_tiles, coded, coded_top, landed, landed_top, local_sem, send, recv):
    region = lax.axis_index("region")
    view = lax.axis_index("view")
    y, x = lax.div(region, 8), lax.rem(lax.div(region, 2), 4)
    z, core = lax.div(view, 2) * 2 + lax.rem(region, 2), lax.rem(view, 2)
    sibling = device(x, y, z, 1 - core)

    def first(step):
        return device(x + (1 - core) * step, y + core * step, z, core)

    def second(step):
        return device(x + core * step, y + (1 - core) * step, z, core)

    def line(step):
        return device(x, y, z + step, core)

    fetches = [
        pltpu.make_async_copy(x_ref, keys.at[pl.ds(0, B)], local_sem.at[0]),
        pltpu.make_async_copy(ids_ref, own_ids.at[0], local_sem.at[1]),
        pltpu.make_async_copy(tiles_ref, own_ids.at[1], local_sem.at[2]),
    ]
    for fetch in fetches:
        fetch.start()
    barrier = pltpu.get_barrier_semaphore()
    peers = [sibling] + [go(step) for go in (first, second, line) for step in (1, -1)]
    for peer in peers:
        pl.semaphore_signal(barrier, inc=1, device_id=peer, device_id_type=MESH)
    for fetch in fetches:
        fetch.wait()
    for part in range(2):
        for held in (key_meta.at[0, part], line_meta.at[3, part]):
            held[0:1, :] = own_ids[0, part:part + 1, :]
            held[1:2, :] = own_ids[1, part:part + 1, :]
    pl.semaphore_wait(barrier, len(peers))

    copies = {}

    def start(name, src, dst, target):
        index = len(copies)
        copies[name] = pltpu.make_async_remote_copy(
            src_ref=src, dst_ref=dst, send_sem=send.at[index], recv_sem=recv.at[index],
            device_id=target, device_id_type=MESH,
        )
        copies[name].start()

    def arrived(*names):
        for name in names:
            copies[name].wait_recv()

    def slot(rel, whose=0, begin=0, count=B):
        return keys.at[pl.ds(place(SLOT[rel], whose, begin), count)]

    def meta(rel, whose=0):
        return key_meta.at[2 * SLOT[rel] + whose]

    def moved(rel, axis, step):
        return tuple((r - step * (i == axis)) % 4 for i, r in enumerate(rel))

    def ids_on(rel, axis, step):
        start(("m", axis, step, rel), meta(rel), meta(moved(rel, axis, step)), (first, second)[axis](step))

    def send_on(rel, axis, step, part=None):
        begin, count = (0, B) if part is None else (part * H, H)
        start(("w", axis, step, rel, part), slot(rel, 0, begin, count),
              slot(moved(rel, axis, step), 0, begin, count), (first, second)[axis](step))

    def came(axis, rel, part=None):
        if rel[axis] == 2:
            step = 1 if part == 0 else -1
        else:
            step = 1 if rel[axis] == 3 else -1
        arrived(("w", axis, step, moved(rel, axis, -step), part))

    def ids_came(axis, *rels):
        for rel in rels:
            step = -1 if rel[axis] == 1 else 1
            arrived(("m", axis, step, moved(rel, axis, -step)))

    def share(rel, part=None):
        begin, count = (0, B) if part is None else (part * H, H)
        start(("s", rel, part), slot(rel, 0, begin, count), slot(rel, 1, begin, count), sibling)

    def share_ids(*rels):
        for rel in rels:
            start(("ms", rel), meta(rel), meta(rel, 1), sibling)

    def shared(*wanted):
        for want in wanted:
            rel, parts = (want[0], (want[1],)) if isinstance(want[0], tuple) else (want, (0, 1))
            if 0 in parts:
                arrived(("ms", rel))
            arrived(*[("s", rel, part) for part in (*parts, None) if ("s", rel, part) in copies])
            for whose in range(2):
                at = 2 * SLOT[rel] + whose
                for part in parts:
                    key_ids[0:2, pl.ds(place(SLOT[rel], whose, part * H), H)] = key_meta[at, part]

    here = (0, 0)
    for axis in (0, 1):
        for step in (1, -1):
            ids_on(here, axis, step)
    start("mu", line_meta.at[3], line_meta.at[2], line(1))
    start("md", line_meta.at[3], line_meta.at[1], line(-1))
    for part in range(2):
        for axis in (0, 1):
            for step in (1, -1):
                send_on(here, axis, step, part)
        at = pl.ds(part * H, H)
        start(("ru", part), keys.at[at], rows.at[pl.ds(DOWN[part], H)], line(1))
        start(("rd", part), keys.at[at], rows.at[pl.ds(UP[part], H)], line(-1))
    share_ids(here)
    share(here)
    rows[OWN[0]:OWN[0] + B, :] = keys[0:B, :]
    acc[...] = jnp.zeros_like(acc)

    def label_rows(*blocks):
        for block in blocks:
            for part in range(2):
                at = pl.ds(LINE[block][part], H)
                held = line_meta[block, part]
                row_ids[at, :] = jnp.broadcast_to(held[0:1, :], (H, H)).T
                row_tiles[at, :] = jnp.broadcast_to(held[1:2, :], (H, H)).T

    half_scale = scale_ref[0] * (0.5 / math.sqrt(D))
    half_bias = bias_ref[0] * 0.5

    def work(row, begin, end, diagonal=False):
        at, cols = pl.ds(row, B), pl.ds(begin, end - begin)
        block = keys[cols, :]
        logits = lax.dot_general(rows[at, :], block, NT, preferred_element_type=jnp.float32)
        curve = jnp.tanh(logits * half_scale + half_bias)
        same = row_ids[at, :][:, 0:1] == key_ids[0:1, cols]
        if diagonal:
            same &= lax.broadcasted_iota(jnp.int32, curve.shape, 0) != lax.broadcasted_iota(jnp.int32, curve.shape, 1)
        near = row_tiles[at, :][:, 0:1] == key_ids[1:2, cols]
        slope = curve + jnp.where(same, -1.0, 1.0)
        slope = jnp.where(near & ~same, 0.0, slope).astype(jnp.bfloat16)
        acc[at, :] += jnp.dot(slope, block, preferred_element_type=jnp.float32)

    def pass_on(piece, row, step):
        sums = acc[pl.ds(row, H), :].reshape(H // 8, 8, D)
        top = jnp.maximum(jnp.max(jnp.abs(sums), axis=0), 1e-30)
        coded_top[piece] = top
        code = jnp.floor(sums * (32767.0 / top)[None] + 0.5).astype(jnp.int32)
        coded[piece] = code.reshape(H, D).astype(jnp.int16)
        start(("t", piece), coded_top.at[piece], landed_top.at[piece], line(step))
        start(("q", piece), coded.at[piece], landed.at[piece], line(step))

    def decoded(piece):
        arrived(("t", piece), ("q", piece))
        sums = landed[piece].astype(jnp.int32).astype(jnp.float32).reshape(H // 8, 8, D)
        return (sums * (landed_top[piece] * (1.0 / 32767.0))[None]).reshape(H, D)

    def take_in(piece, row):
        acc[pl.ds(row, H), :] += decoded(piece)

    def pair(k):
        return SLOTS[k], SLOTS[k + 1]

    def two_hops(rel):
        ids_came(1, rel)
        share_ids(rel)
        for part in range(2):
            came(1, rel, part)
            share(rel, part)

    def beside(rel):
        up, down = (rel, 3), (rel, 1)
        ids_came(1, up, down)
        ids_on(up, 1, 1)
        parts = [None] if rel == 2 else [0, 1]
        for part in parts:
            came(1, up, part)
        send_on(up, 1, 1, 0)
        for part in parts:
            came(1, down, part)
        send_on(down, 1, -1, 1)
        share_ids(down, up)
        share(down)
        share(up)

    def unit(k):
        return 2 * B * k

    opp, near, far, own = 0, B, 2 * B, 3 * B
    near_keys, far_keys = unit(3), unit(5)

    label_rows(3)
    shared(here)
    work(own, 0, unit(1), diagonal=True)

    ids_came(0, *pair(1))
    for rel in pair(1):
        came(0, rel, 0)
    send_on((3, 0), 0, 1, 0)
    for rel in pair(1):
        for step in (1, -1):
            ids_on(rel, 1, step)
            send_on(rel, 1, step, 0)
    ids_on((3, 0), 0, 1)
    ids_came(1, *pair(3))
    for rel in pair(3):
        came(1, rel, 0)
    share_ids(*SLOTS[1:5])
    for rel in SLOTS[1:5]:
        share(rel, 0)
    arrived("mu", "md")
    start("mo", line_meta.at[2], line_meta.at[0], line(1))
    arrived(("ru", 0), ("rd", 0))
    start("ou", rows.at[pl.ds(DOWN[0], H)], rows.at[pl.ds(OPP[0], H)], line(1))
    label_rows(1, 2)
    shared(*[(rel, 0) for rel in SLOTS[1:5]])
    work(near, 0, near_keys)

    for rel in pair(1):
        came(0, rel, 1)
    send_on((1, 0), 0, -1, 1)
    for rel in pair(1):
        for step in (1, -1):
            send_on(rel, 1, step, 1)
    for rel in pair(3):
        came(1, rel, 1)
    for rel in SLOTS[1:5]:
        share(rel, 1)
    arrived(("ru", 1), ("rd", 1))
    start("od", rows.at[pl.ds(UP[1], H)], rows.at[pl.ds(OPP[1], H)], line(-1))
    work(own, unit(1), near_keys)
    shared(*[(rel, 1) for rel in SLOTS[1:5]])
    work(near, near_keys, far_keys)
    work(far, 0, far_keys)

    def others(k, count):
        for row in (opp, near, far):
            work(row, unit(k), unit(k + count))

    ids_came(0, (2, 0))
    for part in range(2):
        came(0, (2, 0), part)
    for step in (1, -1):
        ids_on((2, 0), 1, step)
        send_on((2, 0), 1, step)
    ids_on((0, 3), 1, 1)
    send_on((0, 3), 1, 1, 0)
    send_on((0, 1), 1, -1, 1)
    share_ids((2, 0))
    share((2, 0))
    arrived("mo", "ou", "od")
    label_rows(0)
    work(opp, 0, far_keys)
    beside(1)
    work(own, near_keys, far_keys)
    beside(3)
    shared(*SLOTS[5:8])
    others(5, 3)
    beside(2)
    shared(*pair(8))
    others(8, 2)
    two_hops((0, 2))
    shared(*pair(10))
    others(10, 2)
    two_hops((1, 2))
    two_hops((3, 2))
    shared(*pair(12))
    work(opp, unit(12), unit(14))
    two_hops((2, 2))
    shared((3, 2))
    work(opp, unit(14), unit(15))
    shared((2, 2))

    work(opp, unit(15), unit(16))
    pass_on(0, OPP[0], 1)
    pass_on(1, OPP[1], -1)
    work(near, unit(12), unit(16))
    work(far, unit(12), unit(16))
    pass_on(2, UP[1], 1)
    pass_on(3, DOWN[0], -1)
    work(own, unit(5), unit(11))
    take_in(0, UP[0])
    pass_on(4, UP[0], 1)
    take_in(1, DOWN[1])
    pass_on(5, DOWN[1], -1)
    work(own, unit(11), unit(16))
    take_in(2, OWN[1])
    take_in(3, OWN[0])
    out_ref[0:H, :] = acc[OWN[0]:OWN[0] + H, :] + decoded(4)
    out_ref[H:B, :] = acc[OWN[1]:OWN[1] + H, :] + decoded(5)
    for copy in copies.values():
        copy.wait_send()


COPIES = 128


def local(embeddings, region_ids, tile_ids, logit_scale, logit_bias):
    hbm, vmem, smem = (pl.BlockSpec(memory_space=space) for space in (pltpu.HBM, pltpu.VMEM, pltpu.SMEM))
    sums = pl.pallas_call(
        kernel,
        out_shape=jax.ShapeDtypeStruct((B, D), jnp.float32),
        in_specs=[hbm, hbm, hbm, smem, smem],
        out_specs=vmem,
        scratch_shapes=[
            pltpu.VMEM((2, 2, H), jnp.int32),
            pltpu.VMEM((32 * B, D), jnp.bfloat16),
            pltpu.VMEM((4 * B, D), jnp.bfloat16),
            pltpu.VMEM((4 * B, D), jnp.float32),
            pltpu.VMEM((32, 2, 2, H), jnp.int32),
            pltpu.VMEM((4, 2, 2, H), jnp.int32),
            pltpu.VMEM((8, 32 * B), jnp.int32),
            pltpu.VMEM((4 * B, H), jnp.int32),
            pltpu.VMEM((4 * B, H), jnp.int32),
            pltpu.VMEM((6, H, D), jnp.int16),
            pltpu.VMEM((6, 8, D), jnp.float32),
            pltpu.VMEM((6, H, D), jnp.int16),
            pltpu.VMEM((6, 8, D), jnp.float32),
            pltpu.SemaphoreType.DMA((3,)),
            pltpu.SemaphoreType.DMA((COPIES,)),
            pltpu.SemaphoreType.DMA((COPIES,)),
        ],
        compiler_params=pltpu.CompilerParams(
            collective_id=0, has_side_effects=True, vmem_limit_bytes=36 * 1024 * 1024
        ),
        name="pair_gradients",
    )(embeddings, region_ids.reshape(2, H), tile_ids.reshape(2, H), logit_scale, logit_bias)
    return sums * (logit_scale[0] * (1.0 / math.sqrt(D)))


def solution(mesh):
    placed = (P(("region", "view"), None), P(("region", "view")), P(("region", "view")), P(), P())
    return jax.shard_map(
        local, mesh=mesh, in_specs=placed, out_specs=P(("region", "view"), None), check_vma=False
    )
```

```python
import functools
import math

import jax
import jax.numpy as jnp
from jax import lax
from jax.experimental import pallas as pl
from jax.experimental.pallas import tpu as pltpu
from jax.sharding import PartitionSpec as P

D = 768
B = 256
H = B // 2
MESH = pl.DeviceIdType.MESH
NT = (((1,), (1,)), ((), ()))

SLOTS = [(0, 0), (1, 0), (3, 0), (0, 1), (0, 3), (2, 0), (1, 1), (1, 3)]
SLOTS += [(3, 1), (3, 3), (2, 1), (2, 3), (0, 2), (1, 2), (3, 2), (2, 2)]
SLOT = {rel: k for k, rel in enumerate(SLOTS)}

OPP, UP, DOWN, OWN = (0, H), (B, 2 * B), (B + H, 2 * B + H), (3 * B, 3 * B + H)
LINE = (OPP, UP, DOWN, OWN)


def place(k, whose, begin=0):
    if 1 <= k <= 4:
        return 2 * B + begin * 8 + (k - 1) * B + whose * H
    return (2 * k + whose) * B + begin


def wrap(value):
    return lax.rem(value + 4, 4)


def device(x, y, z, core):
    x, y, z = wrap(x), wrap(y), wrap(z)
    return ((y * 4 + x) * 2 + lax.rem(z, 2), lax.div(z, 2) * 2 + core)


def kernel(x_ref, ids_ref, tiles_ref, scale_ref, bias_ref, out_ref, own_ids, keys, rows, acc, key_meta, line_meta,
           key_ids, row_ids, row_tiles, coded, coded_top, landed, landed_top, local_sem, send, recv):
    region = lax.axis_index("region")
    view = lax.axis_index("view")
    y, x = lax.div(region, 8), lax.rem(lax.div(region, 2), 4)
    z, core = lax.div(view, 2) * 2 + lax.rem(region, 2), lax.rem(view, 2)
    sibling = device(x, y, z, 1 - core)

    def first(step):
        return device(x + (1 - core) * step, y + core * step, z, core)

    def second(step):
        return device(x + core * step, y + (1 - core) * step, z, core)

    def line(step):
        return device(x, y, z + step, core)

    fetches = [
        pltpu.make_async_copy(x_ref, keys.at[pl.ds(0, B)], local_sem.at[0]),
        pltpu.make_async_copy(ids_ref, own_ids.at[0], local_sem.at[1]),
        pltpu.make_async_copy(tiles_ref, own_ids.at[1], local_sem.at[2]),
    ]
    for fetch in fetches:
        fetch.start()
    barrier = pltpu.get_barrier_semaphore()
    peers = [sibling] + [go(step) for go in (first, second, line) for step in (1, -1)]
    for peer in peers:
        pl.semaphore_signal(barrier, inc=1, device_id=peer, device_id_type=MESH)
    for fetch in fetches:
        fetch.wait()
    for part in range(2):
        for held in (key_meta.at[0, part], line_meta.at[3, part]):
            held[0:1, :] = own_ids[0, part:part + 1, :]
            held[1:2, :] = own_ids[1, part:part + 1, :]
    pl.semaphore_wait(barrier, len(peers))

    copies = {}

    def start(name, src, dst, target):
        index = len(copies)
        copies[name] = pltpu.make_async_remote_copy(
            src_ref=src, dst_ref=dst, send_sem=send.at[index], recv_sem=recv.at[index],
            device_id=target, device_id_type=MESH,
        )
        copies[name].start()

    def arrived(*names):
        for name in names:
            copies[name].wait_recv()

    def slot(rel, whose=0, begin=0, count=B):
        return keys.at[pl.ds(place(SLOT[rel], whose, begin), count)]

    def meta(rel, whose=0):
        return key_meta.at[2 * SLOT[rel] + whose]

    def moved(rel, axis, step):
        return tuple((r - step * (i == axis)) % 4 for i, r in enumerate(rel))

    def ids_on(rel, axis, step):
        start(("m", axis, step, rel), meta(rel), meta(moved(rel, axis, step)), (first, second)[axis](step))

    def send_on(rel, axis, step, part=None):
        begin, count = (0, B) if part is None else (part * H, H)
        start(("w", axis, step, rel, part), slot(rel, 0, begin, count),
              slot(moved(rel, axis, step), 0, begin, count), (first, second)[axis](step))

    def came(axis, rel, part=None):
        if rel[axis] == 2:
            step = 1 if part == 0 else -1
        else:
            step = 1 if rel[axis] == 3 else -1
        arrived(("w", axis, step, moved(rel, axis, -step), part))

    def ids_came(axis, *rels):
        for rel in rels:
            step = -1 if rel[axis] == 1 else 1
            arrived(("m", axis, step, moved(rel, axis, -step)))

    def share(rel, part=None):
        begin, count = (0, B) if part is None else (part * H, H)
        start(("s", rel, part), slot(rel, 0, begin, count), slot(rel, 1, begin, count), sibling)

    def share_ids(*rels):
        for rel in rels:
            start(("ms", rel), meta(rel), meta(rel, 1), sibling)

    def shared(*wanted):
        for want in wanted:
            rel, parts = (want[0], (want[1],)) if isinstance(want[0], tuple) else (want, (0, 1))
            if 0 in parts:
                arrived(("ms", rel))
            arrived(*[("s", rel, part) for part in (*parts, None) if ("s", rel, part) in copies])
            for whose in range(2):
                at = 2 * SLOT[rel] + whose
                for part in parts:
                    key_ids[0:2, pl.ds(place(SLOT[rel], whose, part * H), H)] = key_meta[at, part]

    here = (0, 0)
    for axis in (0, 1):
        for step in (1, -1):
            ids_on(here, axis, step)
    start("mu", line_meta.at[3], line_meta.at[2], line(1))
    start("md", line_meta.at[3], line_meta.at[1], line(-1))
    for part in range(2):
        for axis in (0, 1):
            for step in (1, -1):
                send_on(here, axis, step, part)
        at = pl.ds(part * H, H)
        start(("ru", part), keys.at[at], rows.at[pl.ds(DOWN[part], H)], line(1))
        start(("rd", part), keys.at[at], rows.at[pl.ds(UP[part], H)], line(-1))
    share_ids(here)
    share(here)
    rows[OWN[0]:OWN[0] + B, :] = keys[0:B, :]
    acc[...] = jnp.zeros_like(acc)

    def label_rows(*blocks):
        for block in blocks:
            for part in range(2):
                at = pl.ds(LINE[block][part], H)
                held = line_meta[block, part]
                row_ids[at, :] = jnp.broadcast_to(held[0:1, :], (H, H)).T
                row_tiles[at, :] = jnp.broadcast_to(held[1:2, :], (H, H)).T

    half_scale = scale_ref[0] * (0.5 / math.sqrt(D))
    half_bias = bias_ref[0] * 0.5

    def work(row, begin, end, diagonal=False):
        at, cols = pl.ds(row, B), pl.ds(begin, end - begin)
        block = keys[cols, :]
        logits = lax.dot_general(rows[at, :], block, NT, preferred_element_type=jnp.float32)
        curve = jnp.tanh(logits * half_scale + half_bias)
        same = row_ids[at, :][:, 0:1] == key_ids[0:1, cols]
        if diagonal:
            same &= lax.broadcasted_iota(jnp.int32, curve.shape, 0) != lax.broadcasted_iota(jnp.int32, curve.shape, 1)
        near = row_tiles[at, :][:, 0:1] == key_ids[1:2, cols]
        slope = curve + jnp.where(same, -1.0, 1.0)
        slope = jnp.where(near & ~same, 0.0, slope).astype(jnp.bfloat16)
        acc[at, :] += jnp.dot(slope, block, preferred_element_type=jnp.float32)

    def pass_on(piece, row, step):
        sums = acc[pl.ds(row, H), :]
        top = jnp.maximum(jnp.max(jnp.abs(sums), axis=0, keepdims=True), 1e-30)
        coded_top[piece] = top
        coded[piece] = jnp.floor(sums * (32767.0 / top) + 0.5).astype(jnp.int32).astype(jnp.int16)
        start(("t", piece), coded_top.at[piece], landed_top.at[piece], line(step))
        start(("q", piece), coded.at[piece], landed.at[piece], line(step))

    def decoded(piece):
        arrived(("t", piece), ("q", piece))
        return landed[piece].astype(jnp.int32).astype(jnp.float32) * (landed_top[piece] * (1.0 / 32767.0))

    def take_in(piece, row):
        acc[pl.ds(row, H), :] += decoded(piece)

    def pair(k):
        return SLOTS[k], SLOTS[k + 1]

    def two_hops(rel):
        ids_came(1, rel)
        share_ids(rel)
        for part in range(2):
            came(1, rel, part)
            share(rel, part)

    def beside(rel):
        up, down = (rel, 3), (rel, 1)
        ids_came(1, up, down)
        ids_on(up, 1, 1)
        parts = [None] if rel == 2 else [0, 1]
        for part in parts:
            came(1, up, part)
        send_on(up, 1, 1, 0)
        for part in parts:
            came(1, down, part)
        send_on(down, 1, -1, 1)
        share_ids(down, up)
        share(down)
        share(up)

    def unit(k):
        return 2 * B * k

    opp, near, far, own = 0, B, 2 * B, 3 * B
    near_keys, far_keys = unit(3), unit(5)

    label_rows(3)
    shared(here)
    work(own, 0, unit(1), diagonal=True)

    ids_came(0, *pair(1))
    for rel in pair(1):
        came(0, rel, 0)
    send_on((3, 0), 0, 1, 0)
    for rel in pair(1):
        for step in (1, -1):
            ids_on(rel, 1, step)
            send_on(rel, 1, step, 0)
    ids_on((3, 0), 0, 1)
    ids_came(1, *pair(3))
    for rel in pair(3):
        came(1, rel, 0)
    share_ids(*SLOTS[1:5])
    for rel in SLOTS[1:5]:
        share(rel, 0)
    arrived("mu", "md")
    start("mo", line_meta.at[2], line_meta.at[0], line(1))
    arrived(("ru", 0), ("rd", 0))
    start("ou", rows.at[pl.ds(DOWN[0], H)], rows.at[pl.ds(OPP[0], H)], line(1))
    label_rows(1, 2)
    shared(*[(rel, 0) for rel in SLOTS[1:5]])
    work(near, 0, near_keys)

    for rel in pair(1):
        came(0, rel, 1)
    send_on((1, 0), 0, -1, 1)
    for rel in pair(1):
        for step in (1, -1):
            send_on(rel, 1, step, 1)
    for rel in pair(3):
        came(1, rel, 1)
    for rel in SLOTS[1:5]:
        share(rel, 1)
    arrived(("ru", 1), ("rd", 1))
    start("od", rows.at[pl.ds(UP[1], H)], rows.at[pl.ds(OPP[1], H)], line(-1))
    work(own, unit(1), near_keys)
    shared(*[(rel, 1) for rel in SLOTS[1:5]])
    work(near, near_keys, far_keys)
    work(far, 0, far_keys)

    def others(k, count):
        for row in (opp, near, far):
            work(row, unit(k), unit(k + count))

    ids_came(0, (2, 0))
    for part in range(2):
        came(0, (2, 0), part)
    for step in (1, -1):
        ids_on((2, 0), 1, step)
        send_on((2, 0), 1, step)
    ids_on((0, 3), 1, 1)
    send_on((0, 3), 1, 1, 0)
    send_on((0, 1), 1, -1, 1)
    share_ids((2, 0))
    share((2, 0))
    arrived("mo", "ou", "od")
    label_rows(0)
    work(opp, 0, far_keys)
    beside(1)
    work(own, near_keys, far_keys)
    beside(3)
    shared(*SLOTS[5:8])
    others(5, 3)
    beside(2)
    shared(*pair(8))
    others(8, 2)
    two_hops((0, 2))
    shared(*pair(10))
    others(10, 2)
    two_hops((1, 2))
    two_hops((3, 2))
    shared(*pair(12))
    work(opp, unit(12), unit(14))
    two_hops((2, 2))
    shared((3, 2))
    work(opp, unit(14), unit(15))
    shared((2, 2))

    work(opp, unit(15), unit(16))
    pass_on(0, OPP[0], 1)
    pass_on(1, OPP[1], -1)
    work(near, unit(12), unit(16))
    work(far, unit(12), unit(16))
    pass_on(2, UP[1], 1)
    pass_on(3, DOWN[0], -1)
    work(own, unit(5), unit(11))
    take_in(0, UP[0])
    pass_on(4, UP[0], 1)
    take_in(1, DOWN[1])
    pass_on(5, DOWN[1], -1)
    work(own, unit(11), unit(16))
    take_in(2, OWN[1])
    take_in(3, OWN[0])
    out_ref[0:H, :] = acc[OWN[0]:OWN[0] + H, :] + decoded(4)
    out_ref[H:B, :] = acc[OWN[1]:OWN[1] + H, :] + decoded(5)
    for copy in copies.values():
        copy.wait_send()


COPIES = 128


def local(embeddings, region_ids, tile_ids, logit_scale, logit_bias):
    hbm, vmem, smem = (pl.BlockSpec(memory_space=space) for space in (pltpu.HBM, pltpu.VMEM, pltpu.SMEM))
    sums = pl.pallas_call(
        kernel,
        out_shape=jax.ShapeDtypeStruct((B, D), jnp.float32),
        in_specs=[hbm, hbm, hbm, smem, smem],
        out_specs=vmem,
        scratch_shapes=[
            pltpu.VMEM((2, 2, H), jnp.int32),
            pltpu.VMEM((32 * B, D), jnp.bfloat16),
            pltpu.VMEM((4 * B, D), jnp.bfloat16),
            pltpu.VMEM((4 * B, D), jnp.float32),
            pltpu.VMEM((32, 2, 2, H), jnp.int32),
            pltpu.VMEM((4, 2, 2, H), jnp.int32),
            pltpu.VMEM((8, 32 * B), jnp.int32),
            pltpu.VMEM((4 * B, H), jnp.int32),
            pltpu.VMEM((4 * B, H), jnp.int32),
            pltpu.VMEM((6, H, D), jnp.int16),
            pltpu.VMEM((6, 1, D), jnp.float32),
            pltpu.VMEM((6, H, D), jnp.int16),
            pltpu.VMEM((6, 1, D), jnp.float32),
            pltpu.SemaphoreType.DMA((3,)),
            pltpu.SemaphoreType.DMA((COPIES,)),
            pltpu.SemaphoreType.DMA((COPIES,)),
        ],
        compiler_params=pltpu.CompilerParams(
            collective_id=0, has_side_effects=True, vmem_limit_bytes=36 * 1024 * 1024
        ),
        name="pair_gradients",
    )(embeddings, region_ids.reshape(2, H), tile_ids.reshape(2, H), logit_scale, logit_bias)
    return sums * (logit_scale[0] * (1.0 / math.sqrt(D)))


def solution(mesh):
    placed = (P(("region", "view"), None), P(("region", "view")), P(("region", "view")), P(), P())
    return jax.shard_map(
        local, mesh=mesh, in_specs=placed, out_specs=P(("region", "view"), None), check_vma=False
    )
```

```python
import functools
import math

import jax
import jax.numpy as jnp
from jax import lax
from jax.experimental import pallas as pl
from jax.experimental.pallas import tpu as pltpu
from jax.sharding import PartitionSpec as P

D = 768
B = 256
H = B // 2
MESH = pl.DeviceIdType.MESH
NT = (((1,), (1,)), ((), ()))

SLOTS = [(0, 0), (1, 0), (3, 0), (0, 1), (0, 3), (2, 0), (1, 1), (1, 3)]
SLOTS += [(3, 1), (3, 3), (2, 1), (2, 3), (0, 2), (1, 2), (3, 2), (2, 2)]
SLOT = {rel: k for k, rel in enumerate(SLOTS)}

OPP, UP, DOWN, OWN = (0, H), (B, 2 * B), (B + H, 2 * B + H), (3 * B, 3 * B + H)
LINE = (OPP, UP, DOWN, OWN)


def place(k, whose, begin=0):
    if 1 <= k <= 4:
        return 2 * B + begin * 8 + (k - 1) * B + whose * H
    return (2 * k + whose) * B + begin


def wrap(value):
    return lax.rem(value + 4, 4)


def device(x, y, z, core):
    x, y, z = wrap(x), wrap(y), wrap(z)
    return ((y * 4 + x) * 2 + lax.rem(z, 2), lax.div(z, 2) * 2 + core)


def kernel(x_ref, ids_ref, tiles_ref, scale_ref, bias_ref, out_ref, own_ids, keys, rows, acc, key_meta, line_meta,
           key_ids, row_ids, row_tiles, coded, coded_top, landed, landed_top, local_sem, send, recv):
    region = lax.axis_index("region")
    view = lax.axis_index("view")
    y, x = lax.div(region, 8), lax.rem(lax.div(region, 2), 4)
    z, core = lax.div(view, 2) * 2 + lax.rem(region, 2), lax.rem(view, 2)
    sibling = device(x, y, z, 1 - core)

    def first(step):
        return device(x + (1 - core) * step, y + core * step, z, core)

    def second(step):
        return device(x + core * step, y + (1 - core) * step, z, core)

    def line(step):
        return device(x, y, z + step, core)

    fetches = [
        pltpu.make_async_copy(x_ref, keys.at[pl.ds(0, B)], local_sem.at[0]),
        pltpu.make_async_copy(ids_ref, own_ids.at[0], local_sem.at[1]),
        pltpu.make_async_copy(tiles_ref, own_ids.at[1], local_sem.at[2]),
    ]
    for fetch in fetches:
        fetch.start()
    barrier = pltpu.get_barrier_semaphore()
    peers = [sibling] + [go(step) for go in (first, second, line) for step in (1, -1)]
    for peer in peers:
        pl.semaphore_signal(barrier, inc=1, device_id=peer, device_id_type=MESH)
    for fetch in fetches:
        fetch.wait()
    for part in range(2):
        for held in (key_meta.at[0, part], line_meta.at[3, part]):
            held[0:1, :] = own_ids[0, part:part + 1, :]
            held[1:2, :] = own_ids[1, part:part + 1, :]
    pl.semaphore_wait(barrier, len(peers))

    copies = {}

    def start(name, src, dst, target):
        index = len(copies)
        copies[name] = pltpu.make_async_remote_copy(
            src_ref=src, dst_ref=dst, send_sem=send.at[index], recv_sem=recv.at[index],
            device_id=target, device_id_type=MESH,
        )
        copies[name].start()

    def arrived(*names):
        for name in names:
            copies[name].wait_recv()

    def slot(rel, whose=0, begin=0, count=B):
        return keys.at[pl.ds(place(SLOT[rel], whose, begin), count)]

    def meta(rel, whose=0):
        return key_meta.at[2 * SLOT[rel] + whose]

    def moved(rel, axis, step):
        return tuple((r - step * (i == axis)) % 4 for i, r in enumerate(rel))

    def ids_on(rel, axis, step):
        start(("m", axis, step, rel), meta(rel), meta(moved(rel, axis, step)), (first, second)[axis](step))

    def send_on(rel, axis, step, part=None):
        begin, count = (0, B) if part is None else (part * H, H)
        start(("w", axis, step, rel, part), slot(rel, 0, begin, count),
              slot(moved(rel, axis, step), 0, begin, count), (first, second)[axis](step))

    def came(axis, rel, part=None):
        if rel[axis] == 2:
            step = 1 if part == 0 else -1
        else:
            step = 1 if rel[axis] == 3 else -1
        arrived(("w", axis, step, moved(rel, axis, -step), part))

    def ids_came(axis, *rels):
        for rel in rels:
            step = -1 if rel[axis] == 1 else 1
            arrived(("m", axis, step, moved(rel, axis, -step)))

    def share(rel, part=None):
        begin, count = (0, B) if part is None else (part * H, H)
        start(("s", rel, part), slot(rel, 0, begin, count), slot(rel, 1, begin, count), sibling)

    def share_ids(*rels):
        for rel in rels:
            start(("ms", rel), meta(rel), meta(rel, 1), sibling)

    def shared(*wanted):
        for want in wanted:
            rel, parts = (want[0], (want[1],)) if isinstance(want[0], tuple) else (want, (0, 1))
            if 0 in parts:
                arrived(("ms", rel))
            arrived(*[("s", rel, part) for part in (*parts, None) if ("s", rel, part) in copies])
            for whose in range(2):
                at = 2 * SLOT[rel] + whose
                for part in parts:
                    key_ids[0:2, pl.ds(place(SLOT[rel], whose, part * H), H)] = key_meta[at, part]

    here = (0, 0)
    for axis in (0, 1):
        for step in (1, -1):
            ids_on(here, axis, step)
    start("mu", line_meta.at[3], line_meta.at[2], line(1))
    start("md", line_meta.at[3], line_meta.at[1], line(-1))
    for part in range(2):
        for axis in (0, 1):
            for step in (1, -1):
                send_on(here, axis, step, part)
        at = pl.ds(part * H, H)
        start(("ru", part), keys.at[at], rows.at[pl.ds(DOWN[part], H)], line(1))
        start(("rd", part), keys.at[at], rows.at[pl.ds(UP[part], H)], line(-1))
    share_ids(here)
    share(here)
    rows[OWN[0]:OWN[0] + B, :] = keys[0:B, :]
    acc[...] = jnp.zeros_like(acc)

    def label_rows(*blocks):
        for block in blocks:
            for part in range(2):
                at = pl.ds(LINE[block][part], H)
                held = line_meta[block, part]
                row_ids[at, :] = jnp.broadcast_to(held[0:1, :], (H, H)).T
                row_tiles[at, :] = jnp.broadcast_to(held[1:2, :], (H, H)).T

    half_scale = scale_ref[0] * (0.5 / math.sqrt(D))
    half_bias = bias_ref[0] * 0.5

    def work(row, begin, end, diagonal=False):
        at, cols = pl.ds(row, B), pl.ds(begin, end - begin)
        block = keys[cols, :]
        logits = lax.dot_general(rows[at, :], block, NT, preferred_element_type=jnp.float32)
        curve = jnp.tanh(logits * half_scale + half_bias)
        same = row_ids[at, :][:, 0:1] == key_ids[0:1, cols]
        if diagonal:
            same &= lax.broadcasted_iota(jnp.int32, curve.shape, 0) != lax.broadcasted_iota(jnp.int32, curve.shape, 1)
        near = row_tiles[at, :][:, 0:1] == key_ids[1:2, cols]
        slope = curve + jnp.where(same, -1.0, 1.0)
        slope = jnp.where(near & ~same, 0.0, slope).astype(jnp.bfloat16)
        acc[at, :] += jnp.dot(slope, block, preferred_element_type=jnp.float32)

    def pass_on(piece, row, step):
        sums = acc[pl.ds(row, H), :]
        top = jnp.maximum(jnp.max(jnp.abs(sums), axis=0, keepdims=True), 1e-30)
        coded_top[piece] = top
        coded[piece] = jnp.floor(sums * (32767.0 / top) + 0.5).astype(jnp.int32).astype(jnp.int16)
        start(("t", piece), coded_top.at[piece], landed_top.at[piece], line(step))
        start(("q", piece), coded.at[piece], landed.at[piece], line(step))

    def decoded(piece):
        arrived(("t", piece), ("q", piece))
        return landed[piece].astype(jnp.int32).astype(jnp.float32) * (landed_top[piece] * (1.0 / 32767.0))

    def take_in(piece, row):
        acc[pl.ds(row, H), :] += decoded(piece)

    def pair(k):
        return SLOTS[k], SLOTS[k + 1]

    def two_hops(rel):
        ids_came(1, rel)
        share_ids(rel)
        for part in range(2):
            came(1, rel, part)
            share(rel, part)

    def beside(rel):
        up, down = (rel, 3), (rel, 1)
        ids_came(1, up, down)
        ids_on(up, 1, 1)
        parts = [None] if rel == 2 else [0, 1]
        for part in parts:
            came(1, up, part)
        send_on(up, 1, 1, 0)
        for part in parts:
            came(1, down, part)
        send_on(down, 1, -1, 1)
        share_ids(down, up)
        share(down)
        share(up)

    def unit(k):
        return 2 * B * k

    opp, near, far, own = 0, B, 2 * B, 3 * B
    near_keys, far_keys = unit(3), unit(5)

    label_rows(3)
    shared(here)
    work(own, 0, unit(1), diagonal=True)

    ids_came(0, *pair(1))
    for rel in pair(1):
        came(0, rel, 0)
    send_on((3, 0), 0, 1, 0)
    for rel in pair(1):
        for step in (1, -1):
            ids_on(rel, 1, step)
            send_on(rel, 1, step, 0)
    ids_on((3, 0), 0, 1)
    ids_came(1, *pair(3))
    for rel in pair(3):
        came(1, rel, 0)
    share_ids(*SLOTS[1:5])
    for rel in SLOTS[1:5]:
        share(rel, 0)
    arrived("mu", "md")
    start("mo", line_meta.at[2], line_meta.at[0], line(1))
    arrived(("ru", 0), ("rd", 0))
    start("ou", rows.at[pl.ds(DOWN[0], H)], rows.at[pl.ds(OPP[0], H)], line(1))
    label_rows(1, 2)
    shared(*[(rel, 0) for rel in SLOTS[1:5]])
    work(near, 0, near_keys)

    for rel in pair(1):
        came(0, rel, 1)
    send_on((1, 0), 0, -1, 1)
    for rel in pair(1):
        for step in (1, -1):
            send_on(rel, 1, step, 1)
    for rel in pair(3):
        came(1, rel, 1)
    for rel in SLOTS[1:5]:
        share(rel, 1)
    arrived(("ru", 1), ("rd", 1))
    start("od", rows.at[pl.ds(UP[1], H)], rows.at[pl.ds(OPP[1], H)], line(-1))
    work(own, unit(1), near_keys)
    shared(*[(rel, 1) for rel in SLOTS[1:5]])
    work(near, near_keys, far_keys)
    work(far, 0, far_keys)

    def others(k, count):
        for row in (opp, near, far):
            work(row, unit(k), unit(k + count))

    ids_came(0, (2, 0))
    for part in range(2):
        came(0, (2, 0), part)
    for step in (1, -1):
        ids_on((2, 0), 1, step)
        send_on((2, 0), 1, step)
    ids_on((0, 3), 1, 1)
    send_on((0, 3), 1, 1, 0)
    send_on((0, 1), 1, -1, 1)
    share_ids((2, 0))
    share((2, 0))
    arrived("mo", "ou", "od")
    label_rows(0)
    work(opp, 0, far_keys)
    beside(1)
    work(own, near_keys, far_keys)
    beside(3)
    shared(*SLOTS[5:8])
    others(5, 3)
    beside(2)
    shared(*pair(8))
    others(8, 2)
    two_hops((0, 2))
    shared(*pair(10))
    others(10, 2)
    two_hops((1, 2))
    two_hops((3, 2))
    shared(*pair(12))
    work(opp, unit(12), unit(14))
    two_hops((2, 2))
    shared((3, 2))
    for part in range(2):
        key_ids[0:2, pl.ds(place(15, 0, part * H), H)] = key_meta[30, part]
    work(opp, unit(14), unit(15) + B)
    work(near, unit(12), unit(14))
    shared((2, 2))

    work(opp, unit(15) + B, unit(16))
    pass_on(0, OPP[0], 1)
    pass_on(1, OPP[1], -1)
    work(near, unit(14), unit(16))
    work(far, unit(12), unit(16))
    pass_on(2, UP[1], 1)
    pass_on(3, DOWN[0], -1)
    work(own, unit(5), unit(9))
    take_in(0, UP[0])
    pass_on(4, UP[0], 1)
    take_in(1, DOWN[1])
    pass_on(5, DOWN[1], -1)
    work(own, unit(9), unit(12))
    work(own, unit(12), unit(16))
    take_in(2, OWN[1])
    take_in(3, OWN[0])
    out_ref[0:H, :] = acc[OWN[0]:OWN[0] + H, :] + decoded(4)
    out_ref[H:B, :] = acc[OWN[1]:OWN[1] + H, :] + decoded(5)
    for copy in copies.values():
        copy.wait_send()


COPIES = 128


def local(embeddings, region_ids, tile_ids, logit_scale, logit_bias):
    hbm, vmem, smem = (pl.BlockSpec(memory_space=space) for space in (pltpu.HBM, pltpu.VMEM, pltpu.SMEM))
    sums = pl.pallas_call(
        kernel,
        out_shape=jax.ShapeDtypeStruct((B, D), jnp.float32),
        in_specs=[hbm, hbm, hbm, smem, smem],
        out_specs=vmem,
        scratch_shapes=[
            pltpu.VMEM((2, 2, H), jnp.int32),
            pltpu.VMEM((32 * B, D), jnp.bfloat16),
            pltpu.VMEM((4 * B, D), jnp.bfloat16),
            pltpu.VMEM((4 * B, D), jnp.float32),
            pltpu.VMEM((32, 2, 2, H), jnp.int32),
            pltpu.VMEM((4, 2, 2, H), jnp.int32),
            pltpu.VMEM((8, 32 * B), jnp.int32),
            pltpu.VMEM((4 * B, H), jnp.int32),
            pltpu.VMEM((4 * B, H), jnp.int32),
            pltpu.VMEM((6, H, D), jnp.int16),
            pltpu.VMEM((6, 1, D), jnp.float32),
            pltpu.VMEM((6, H, D), jnp.int16),
            pltpu.VMEM((6, 1, D), jnp.float32),
            pltpu.SemaphoreType.DMA((3,)),
            pltpu.SemaphoreType.DMA((COPIES,)),
            pltpu.SemaphoreType.DMA((COPIES,)),
        ],
        compiler_params=pltpu.CompilerParams(
            collective_id=0, has_side_effects=True, vmem_limit_bytes=36 * 1024 * 1024
        ),
        name="pair_gradients",
    )(embeddings, region_ids.reshape(2, H), tile_ids.reshape(2, H), logit_scale, logit_bias)
    return sums * (logit_scale[0] * (1.0 / math.sqrt(D)))


def solution(mesh):
    placed = (P(("region", "view"), None), P(("region", "view")), P(("region", "view")), P(), P())
    return jax.shard_map(
        local, mesh=mesh, in_specs=placed, out_specs=P(("region", "view"), None), check_vma=False
    )
```

```python
import functools
import math

import jax
import jax.numpy as jnp
from jax import lax
from jax.experimental import pallas as pl
from jax.experimental.pallas import tpu as pltpu
from jax.sharding import PartitionSpec as P

D = 768
B = 256
H = B // 2
MESH = pl.DeviceIdType.MESH
NT = (((1,), (1,)), ((), ()))

SLOTS = [(0, 0), (1, 0), (3, 0), (0, 1), (0, 3), (2, 0), (1, 1), (1, 3)]
SLOTS += [(3, 1), (3, 3), (2, 1), (2, 3), (0, 2), (1, 2), (3, 2), (2, 2)]
SLOT = {rel: k for k, rel in enumerate(SLOTS)}

OPP, UP, DOWN, OWN = (0, H), (B, 2 * B), (B + H, 2 * B + H), (3 * B, 3 * B + H)
LINE = (OPP, UP, DOWN, OWN)


def place(k, whose, begin=0):
    if 1 <= k <= 4:
        return 2 * B + begin * 8 + (k - 1) * B + whose * H
    return (2 * k + whose) * B + begin


def wrap(value):
    return lax.rem(value + 4, 4)


def device(x, y, z, core):
    x, y, z = wrap(x), wrap(y), wrap(z)
    return ((y * 4 + x) * 2 + lax.rem(z, 2), lax.div(z, 2) * 2 + core)


def kernel(x_ref, ids_ref, tiles_ref, scale_ref, bias_ref, out_ref, own_ids, keys, rows, acc, key_meta, line_meta,
           key_ids, row_ids, row_tiles, coded, coded_top, landed, landed_top, local_sem, send, recv):
    region = lax.axis_index("region")
    view = lax.axis_index("view")
    y, x = lax.div(region, 8), lax.rem(lax.div(region, 2), 4)
    z, core = lax.div(view, 2) * 2 + lax.rem(region, 2), lax.rem(view, 2)
    sibling = device(x, y, z, 1 - core)

    def first(step):
        return device(x + (1 - core) * step, y + core * step, z, core)

    def second(step):
        return device(x + core * step, y + (1 - core) * step, z, core)

    def line(step):
        return device(x, y, z + step, core)

    fetches = [
        pltpu.make_async_copy(x_ref, keys.at[pl.ds(0, B)], local_sem.at[0]),
        pltpu.make_async_copy(ids_ref, own_ids.at[0], local_sem.at[1]),
        pltpu.make_async_copy(tiles_ref, own_ids.at[1], local_sem.at[2]),
    ]
    for fetch in fetches:
        fetch.start()
    barrier = pltpu.get_barrier_semaphore()
    peers = [sibling] + [go(step) for go in (first, second, line) for step in (1, -1)]
    for peer in peers:
        pl.semaphore_signal(barrier, inc=1, device_id=peer, device_id_type=MESH)
    for fetch in fetches:
        fetch.wait()
    for part in range(2):
        for held in (key_meta.at[0, part], line_meta.at[3, part]):
            held[0:1, :] = own_ids[0, part:part + 1, :]
            held[1:2, :] = own_ids[1, part:part + 1, :]
    pl.semaphore_wait(barrier, len(peers))

    copies = {}

    def start(name, src, dst, target):
        index = len(copies)
        copies[name] = pltpu.make_async_remote_copy(
            src_ref=src, dst_ref=dst, send_sem=send.at[index], recv_sem=recv.at[index],
            device_id=target, device_id_type=MESH,
        )
        copies[name].start()

    def arrived(*names):
        for name in names:
            copies[name].wait_recv()

    def slot(rel, whose=0, begin=0, count=B):
        return keys.at[pl.ds(place(SLOT[rel], whose, begin), count)]

    def meta(rel, whose=0):
        return key_meta.at[2 * SLOT[rel] + whose]

    def moved(rel, axis, step):
        return tuple((r - step * (i == axis)) % 4 for i, r in enumerate(rel))

    def ids_on(rel, axis, step):
        start(("m", axis, step, rel), meta(rel), meta(moved(rel, axis, step)), (first, second)[axis](step))

    def send_on(rel, axis, step, part=None):
        begin, count = (0, B) if part is None else (part * H, H)
        start(("w", axis, step, rel, part), slot(rel, 0, begin, count),
              slot(moved(rel, axis, step), 0, begin, count), (first, second)[axis](step))

    def came(axis, rel, part=None):
        if rel[axis] == 2:
            step = 1 if part == 0 else -1
        else:
            step = 1 if rel[axis] == 3 else -1
        arrived(("w", axis, step, moved(rel, axis, -step), part))

    def ids_came(axis, *rels):
        for rel in rels:
            step = -1 if rel[axis] == 1 else 1
            arrived(("m", axis, step, moved(rel, axis, -step)))

    def share(rel, part=None):
        begin, count = (0, B) if part is None else (part * H, H)
        start(("s", rel, part), slot(rel, 0, begin, count), slot(rel, 1, begin, count), sibling)

    def share_ids(*rels):
        for rel in rels:
            start(("ms", rel), meta(rel), meta(rel, 1), sibling)

    def shared(*wanted):
        for want in wanted:
            rel, parts = (want[0], (want[1],)) if isinstance(want[0], tuple) else (want, (0, 1))
            if 0 in parts:
                arrived(("ms", rel))
            arrived(*[("s", rel, part) for part in (*parts, None) if ("s", rel, part) in copies])
            for whose in range(2):
                at = 2 * SLOT[rel] + whose
                for part in parts:
                    key_ids[0:2, pl.ds(place(SLOT[rel], whose, part * H), H)] = key_meta[at, part]

    here = (0, 0)
    for axis in (0, 1):
        for step in (1, -1):
            ids_on(here, axis, step)
    start("mu", line_meta.at[3], line_meta.at[2], line(1))
    start("md", line_meta.at[3], line_meta.at[1], line(-1))
    for part in range(2):
        for axis in (0, 1):
            for step in (1, -1):
                send_on(here, axis, step, part)
        at = pl.ds(part * H, H)
        start(("ru", part), keys.at[at], rows.at[pl.ds(DOWN[part], H)], line(1))
        start(("rd", part), keys.at[at], rows.at[pl.ds(UP[part], H)], line(-1))
    share_ids(here)
    share(here)
    rows[OWN[0]:OWN[0] + B, :] = keys[0:B, :]
    acc[...] = jnp.zeros_like(acc)

    def label_rows(*blocks):
        for block in blocks:
            for part in range(2):
                at = pl.ds(LINE[block][part], H)
                held = line_meta[block, part]
                row_ids[at, :] = jnp.broadcast_to(held[0:1, :], (H, H)).T
                row_tiles[at, :] = jnp.broadcast_to(held[1:2, :], (H, H)).T

    half_scale = scale_ref[0] * (0.5 / math.sqrt(D))
    half_bias = bias_ref[0] * 0.5

    def work(row, begin, end, diagonal=False):
        at, cols = pl.ds(row, B), pl.ds(begin, end - begin)
        block = keys[cols, :]
        logits = lax.dot_general(rows[at, :], block, NT, preferred_element_type=jnp.float32)
        curve = jnp.tanh(logits * half_scale + half_bias)
        same = row_ids[at, :][:, 0:1] == key_ids[0:1, cols]
        if diagonal:
            same &= lax.broadcasted_iota(jnp.int32, curve.shape, 0) != lax.broadcasted_iota(jnp.int32, curve.shape, 1)
        near = row_tiles[at, :][:, 0:1] == key_ids[1:2, cols]
        slope = curve + jnp.where(same, -1.0, 1.0)
        slope = jnp.where(near & ~same, 0.0, slope).astype(jnp.bfloat16)
        acc[at, :] += jnp.dot(slope, block, preferred_element_type=jnp.float32)

    def pass_on(piece, row, step):
        sums = acc[pl.ds(row, H), :]
        top = jnp.maximum(jnp.max(jnp.abs(sums), axis=0, keepdims=True), 1e-30)
        coded_top[piece] = top
        coded[piece] = jnp.floor(sums * (32767.0 / top) + 0.5).astype(jnp.int32).astype(jnp.int16)
        start(("t", piece), coded_top.at[piece], landed_top.at[piece], line(step))
        start(("q", piece), coded.at[piece], landed.at[piece], line(step))

    def decoded(piece):
        arrived(("t", piece), ("q", piece))
        return landed[piece].astype(jnp.int32).astype(jnp.float32) * (landed_top[piece] * (1.0 / 32767.0))

    def take_in(piece, row):
        acc[pl.ds(row, H), :] += decoded(piece)

    def pair(k):
        return SLOTS[k], SLOTS[k + 1]

    def two_hops(rel):
        ids_came(1, rel)
        share_ids(rel)
        for part in range(2):
            came(1, rel, part)
            share(rel, part)

    def beside(rel):
        up, down = (rel, 3), (rel, 1)
        ids_came(1, up, down)
        ids_on(up, 1, 1)
        parts = [None] if rel == 2 else [0, 1]
        for part in parts:
            came(1, up, part)
        send_on(up, 1, 1, 0)
        for part in parts:
            came(1, down, part)
        send_on(down, 1, -1, 1)
        share_ids(down, up)
        share(down)
        share(up)

    def unit(k):
        return 2 * B * k

    opp, near, far, own = 0, B, 2 * B, 3 * B
    near_keys, far_keys = unit(3), unit(5)

    label_rows(3)
    shared(here)
    work(own, 0, unit(1), diagonal=True)

    ids_came(0, *pair(1))
    for rel in pair(1):
        came(0, rel, 0)
    send_on((3, 0), 0, 1, 0)
    for rel in pair(1):
        for step in (1, -1):
            ids_on(rel, 1, step)
            send_on(rel, 1, step, 0)
    ids_on((3, 0), 0, 1)
    ids_came(1, *pair(3))
    for rel in pair(3):
        came(1, rel, 0)
    share_ids(*SLOTS[1:5])
    for rel in SLOTS[1:5]:
        share(rel, 0)
    arrived("mu", "md")
    start("mo", line_meta.at[2], line_meta.at[0], line(1))
    arrived(("ru", 0), ("rd", 0))
    start("ou", rows.at[pl.ds(DOWN[0], H)], rows.at[pl.ds(OPP[0], H)], line(1))
    label_rows(1, 2)
    shared(*[(rel, 0) for rel in SLOTS[1:5]])
    work(near, 0, near_keys)

    for rel in pair(1):
        came(0, rel, 1)
    send_on((1, 0), 0, -1, 1)
    for rel in pair(1):
        for step in (1, -1):
            send_on(rel, 1, step, 1)
    for rel in pair(3):
        came(1, rel, 1)
    for rel in SLOTS[1:5]:
        share(rel, 1)
    arrived(("ru", 1), ("rd", 1))
    start("od", rows.at[pl.ds(UP[1], H)], rows.at[pl.ds(OPP[1], H)], line(-1))
    work(own, unit(1), near_keys)
    shared(*[(rel, 1) for rel in SLOTS[1:5]])
    work(near, near_keys, far_keys)
    work(far, 0, far_keys)

    def others(k, count):
        for row in (opp, near, far):
            work(row, unit(k), unit(k + count))

    ids_came(0, (2, 0))
    for part in range(2):
        came(0, (2, 0), part)
    for step in (1, -1):
        ids_on((2, 0), 1, step)
        send_on((2, 0), 1, step)
    ids_on((0, 3), 1, 1)
    send_on((0, 3), 1, 1, 0)
    send_on((0, 1), 1, -1, 1)
    share_ids((2, 0))
    share((2, 0))
    arrived("mo", "ou", "od")
    label_rows(0)
    work(opp, 0, far_keys)
    beside(1)
    work(own, near_keys, far_keys)
    beside(3)
    shared(*SLOTS[5:8])
    others(5, 3)
    beside(2)
    shared(*pair(8))
    others(8, 2)
    two_hops((0, 2))
    shared(*pair(10))
    others(10, 2)
    two_hops((1, 2))
    shared((0, 2))
    work(opp, unit(12), unit(13))
    two_hops((3, 2))
    shared((1, 2))
    work(opp, unit(13), unit(14))
    two_hops((2, 2))
    shared((3, 2))
    for part in range(2):
        key_ids[0:2, pl.ds(place(15, 0, part * H), H)] = key_meta[30, part]
    work(opp, unit(14), unit(15) + B)
    work(near, unit(12), unit(14))
    shared((2, 2))

    work(opp, unit(15) + B, unit(16))
    pass_on(0, OPP[0], 1)
    pass_on(1, OPP[1], -1)
    work(near, unit(14), unit(16))
    work(far, unit(12), unit(16))
    pass_on(2, UP[1], 1)
    pass_on(3, DOWN[0], -1)
    work(own, unit(5), unit(9))
    take_in(0, UP[0])
    pass_on(4, UP[0], 1)
    take_in(1, DOWN[1])
    pass_on(5, DOWN[1], -1)
    work(own, unit(9), unit(12))
    work(own, unit(12), unit(16))
    take_in(2, OWN[1])
    take_in(3, OWN[0])
    out_ref[0:H, :] = acc[OWN[0]:OWN[0] + H, :] + decoded(4)
    out_ref[H:B, :] = acc[OWN[1]:OWN[1] + H, :] + decoded(5)
    for copy in copies.values():
        copy.wait_send()


COPIES = 128


def local(embeddings, region_ids, tile_ids, logit_scale, logit_bias):
    hbm, vmem, smem = (pl.BlockSpec(memory_space=space) for space in (pltpu.HBM, pltpu.VMEM, pltpu.SMEM))
    sums = pl.pallas_call(
        kernel,
        out_shape=jax.ShapeDtypeStruct((B, D), jnp.float32),
        in_specs=[hbm, hbm, hbm, smem, smem],
        out_specs=vmem,
        scratch_shapes=[
            pltpu.VMEM((2, 2, H), jnp.int32),
            pltpu.VMEM((32 * B, D), jnp.bfloat16),
            pltpu.VMEM((4 * B, D), jnp.bfloat16),
            pltpu.VMEM((4 * B, D), jnp.float32),
            pltpu.VMEM((32, 2, 2, H), jnp.int32),
            pltpu.VMEM((4, 2, 2, H), jnp.int32),
            pltpu.VMEM((8, 32 * B), jnp.int32),
            pltpu.VMEM((4 * B, H), jnp.int32),
            pltpu.VMEM((4 * B, H), jnp.int32),
            pltpu.VMEM((6, H, D), jnp.int16),
            pltpu.VMEM((6, 1, D), jnp.float32),
            pltpu.VMEM((6, H, D), jnp.int16),
            pltpu.VMEM((6, 1, D), jnp.float32),
            pltpu.SemaphoreType.DMA((3,)),
            pltpu.SemaphoreType.DMA((COPIES,)),
            pltpu.SemaphoreType.DMA((COPIES,)),
        ],
        compiler_params=pltpu.CompilerParams(
            collective_id=0, has_side_effects=True, vmem_limit_bytes=36 * 1024 * 1024
        ),
        name="pair_gradients",
    )(embeddings, region_ids.reshape(2, H), tile_ids.reshape(2, H), logit_scale, logit_bias)
    return sums * (logit_scale[0] * (1.0 / math.sqrt(D)))


def solution(mesh):
    placed = (P(("region", "view"), None), P(("region", "view")), P(("region", "view")), P(), P())
    return jax.shard_map(
        local, mesh=mesh, in_specs=placed, out_specs=P(("region", "view"), None), check_vma=False
    )
```
